128 devices in a mesh: exp: 8 (over y, z_hi), gy: 4 (over z_lo, core), gz: 4 (over x).
Axes of the slice: x: 4, y: 4, z: 4 (z_hi: 2, z_lo: 2; z = z_hi * 2 + z_lo), core: 2. Of those that a mesh axis runs over, the one named last changes fastest.
Arguments:
- adjoint_final: float32 [8, 128, 128, 1024], P('exp', None, 'gy', 'gz'), may hold values from -6 to 6
- concentration: bfloat16 [2, 8, 128, 128, 1024], P(None, 'exp', None, 'gy', 'gz'), may hold values from 0 to 1
- observed: bfloat16 [2, 8, 128, 128, 1024], P(None, 'exp', None, 'gy', 'gz'), may hold values from 0 to 1
- capacity: float32 [128, 128, 1024], P(None, 'gy', 'gz'), may hold values from 0.03 to 0.3
- pore_mask: int32 [128, 128, 1024], P(None, 'gy', 'gz'), may hold values 0 or 1
- feed_index: int32 [8], P('exp'), may hold values from 0 to 7
- feed_affinity: float32 [8], replicated, may hold values from 0.5 to 4
Outputs:
- adjoint_first: float32 [8, 128, 128, 1024], P('exp', None, 'gy', 'gz')
- capacity_grad: float32 [128, 128, 1024], P('exp', 'gy', 'gz')
The draws below stay inside these ranges and needn't reach their ends.
All inputs are finite; a program needn't handle non-finite values. No bound on the sum of `pore_mask` on one device may be relied on, other than what follows from the above.
Results may differ from the reference program's by a relative error of at most 0.0003.
Values sent between devices are 32-bit elements; how exact they have to be, the bound alone decides.
No kernel may reach another device: no remote copies, remote signals or barrier semaphores. Data moves between devices by JAX's collectives and lax.ppermute only.
A program may use at most 128 MiB of HBM per device.

```python
import math
import jax
import jax.numpy as jnp
from jax import lax

X = 128
STEPS = 2
FEEDS = 8
EXPS = 8
Y = 128
Z = 1024


def with_ends(values, key, smallest, high):
    longest = values.shape.index(max(values.shape))
    spots = []
    for shift in (0, 1):
        where = [jax.random.randint(jax.random.fold_in(key, axis), (), 0, length) for axis, length in enumerate(values.shape)]
        where[longest] = (where[longest] + shift) % values.shape[longest]
        spots.append(tuple(where))
    return values.at[spots[0]].set(smallest).at[spots[1]].set(high)


def levels(key, extent, split, smallest, top_value):
    gain = 1.0
    for position, blocks in split:
        steps = jax.random.uniform(jax.random.fold_in(jax.random.fold_in(key, 6), position), (blocks,), jnp.float32, smallest / len(split), top_value / len(split))
        gain = gain * jnp.repeat(jnp.exp(steps), extent[position] // blocks).reshape((-1,) + (1,) * (len(extent) - 1 - position))
    return gain


def noise(stream_key, extent, deviation, limit, split=(), held_as=jnp.bfloat16):
    values = deviation * jax.random.normal(stream_key, extent, jnp.float32)
    if split:
        values = values * levels(stream_key, extent, split, -0.22, 0.18)
    return jnp.clip(values, -limit, limit).astype(held_as)


def setup_inputs(seed: int = 0) -> dict:
    keys = jax.random.split(jax.random.key(seed), 8)
    return {
        "adjoint_final": noise(keys[0], (EXPS, X, Y, Z), 1.0, 6.0, ((0, 8), (2, 4), (3, 4)), jnp.float32),
        "concentration": jnp.clip(1.0 * jax.random.uniform(keys[1], (STEPS, EXPS, X, Y, Z), jnp.float32) ** levels(keys[1], (STEPS, EXPS, X, Y, Z), ((1, 8), (3, 4), (4, 4)), -0.2, 0.2), 0.0, 1.0).astype(jnp.bfloat16),
        "observed": jnp.clip(1.0 * jax.random.uniform(keys[2], (STEPS, EXPS, X, Y, Z), jnp.float32) ** levels(keys[2], (STEPS, EXPS, X, Y, Z), ((1, 8), (3, 4), (4, 4)), -0.2, 0.2), 0.0, 1.0).astype(jnp.bfloat16),
        "capacity": jnp.clip(jnp.exp(math.log(0.3) - 2.3025852 * jax.random.uniform(keys[3], (X, Y, Z), jnp.float32) ** levels(keys[3], (X, Y, Z), ((1, 4), (2, 4)), -0.2, 0.2)), 0.03, 0.3),
        "pore_mask": with_ends((jax.random.randint(keys[4], (X, Y, Z), 0, 5) < 3).astype(jnp.int32), jax.random.fold_in(keys[4], 1), 0, 1),
        "feed_index": with_ends(jax.random.randint(keys[5], (EXPS,), 0, FEEDS), jax.random.fold_in(keys[5], 1), 0, FEEDS - 1).astype(jnp.int32),
        "feed_affinity": jnp.clip(jnp.exp(jax.random.uniform(keys[6], (FEEDS,), jnp.float32, math.log(0.5), math.log(4.0))), 0.5, 4.0),
    }


def face_flux(near_adj, near_pores, adjoint):
    return near_pores * (near_adj - adjoint)


def adjoint_update(adjoint_wide, pores_wide, capacity, affinity, filled_low, observed_low):
    adjoint = adjoint_wide[:, 1:-1, 1:-1]
    pores = pores_wide[:, 1:-1, 1:-1]
    adjoint_x = jnp.pad(adjoint, ((1, 1), (0, 0), (0, 0)))
    pores_x = jnp.pad(pores, ((1, 1), (0, 0), (0, 0)))
    dispersion = face_flux(adjoint_x[2:], pores_x[2:], adjoint) + face_flux(adjoint_x[:-2], pores_x[:-2], adjoint)
    dispersion = dispersion + face_flux(adjoint_wide[:, 2:, 1:-1], pores_wide[:, 2:, 1:-1], adjoint)
    dispersion = dispersion + face_flux(adjoint_wide[:, :-2, 1:-1], pores_wide[:, :-2, 1:-1], adjoint)
    dispersion = dispersion + face_flux(adjoint_wide[:, 1:-1, 2:], pores_wide[:, 1:-1, 2:], adjoint)
    dispersion = dispersion + face_flux(adjoint_wide[:, 1:-1, :-2], pores_wide[:, 1:-1, :-2], adjoint)
    pores_next = jnp.concatenate([pores[1:], jnp.ones_like(pores[:1])], 0)
    adjoint_next = jnp.concatenate([adjoint[1:], jnp.zeros_like(adjoint[:1])], 0)
    transport = pores_next * (adjoint_next - adjoint)
    filled = filled_low.astype(jnp.float32)
    saturation = 1.0 + affinity * filled
    uptake = capacity * affinity / (saturation * saturation)
    updated = pores * (adjoint + 0.1 * dispersion + 0.2 * transport - uptake * adjoint
                       + (filled - observed_low.astype(jnp.float32)))
    gradient_term = -pores * affinity * filled / saturation * adjoint
    return updated, gradient_term


def reference(adjoint_final, concentration, observed, capacity, pore_mask, feed_index, feed_affinity):
    pores = pore_mask.astype(jnp.float32)
    pores_wide = jnp.pad(pores, ((0, 0), (1, 1), (1, 1)))
    feeds = jnp.arange(FEEDS, dtype=jnp.int32)

    def one_experiment(inputs):
        adjoint, filled_all, observed_all, which = inputs
        affinity = jnp.sum(jnp.where(feeds == which, feed_affinity, jnp.zeros_like(feed_affinity)))
        gradient = jnp.zeros_like(adjoint)
        for moment in reversed(range(STEPS)):
            adjoint_wide = jnp.pad(adjoint, ((0, 0), (1, 1), (1, 1)))
            adjoint, gradient_term = adjoint_update(adjoint_wide, pores_wide, capacity, affinity,
                                                    filled_all[moment], observed_all[moment])
            gradient = gradient + gradient_term
        return adjoint, gradient

    adjoint_first, gradients = lax.map(one_experiment, (adjoint_final, jnp.swapaxes(concentration, 0, 1),
                                                        jnp.swapaxes(observed, 0, 1), feed_index))
    return adjoint_first, jnp.sum(gradients, axis=0)
```

```python
import functools

import jax
import jax.numpy as jnp
from jax import lax
from jax.experimental import pallas as pl
from jax.experimental.pallas import tpu as pltpu
from jax.sharding import PartitionSpec as P

F32 = jnp.float32
VMEM_LIMIT = 40 * 1024 * 1024


def reciprocal(value):
    guess = pl.reciprocal(value, approx=True)
    return guess * (2.0 - value * guess)


def lane_to(values, source, target):
    lanes = values.shape[1]
    shift = target - source
    if isinstance(shift, int):
        return pltpu.roll(values, shift % lanes, 1)
    return pltpu.roll(values, lax.rem(shift + lanes, lanes), 1)


def beside_sum(centre, y_low, y_high, z_low, z_high):
    ny, nz = centre.shape
    row = lax.broadcasted_iota(jnp.int32, (ny, nz), 0)
    col = lax.broadcasted_iota(jnp.int32, (ny, nz), 1)
    reps = nz // z_low.shape[1]
    z_low = jnp.concatenate([z_low] * reps, 1)
    z_high = jnp.concatenate([z_high] * reps, 1)
    total = jnp.where(row == 0, y_low, pltpu.roll(centre, 1, 0))
    total = total + jnp.where(row == ny - 1, y_high, pltpu.roll(centre, ny - 1, 0))
    total = total + jnp.where(col == 0, z_low, pltpu.roll(centre, 1, 1))
    return total + jnp.where(col == nz - 1, z_high, pltpu.roll(centre, nz - 1, 1))


def window(start, planes, nx):
    return jnp.clip(start - 1, 0, nx - planes - 2)


def gather_window(start, planes, nx, adj_ref, pore_ref, m_scr, p_scr, masked):
    base = window(start, planes, nx)

    def body(j, _):
        x = start - 1 + j
        at = jnp.clip(x - base, 0, planes + 1)
        inside = jnp.logical_and(x >= 0, x < nx).astype(F32)
        pores = pore_ref[at].astype(F32) * inside
        p_scr[j] = pores
        m_scr[j] = adj_ref[at] * (inside if masked else pores)
        return 0

    lax.fori_loop(0, planes + 2, body, 0)


def halo_column(ref, part, rows, x, target):
    values = ref[part * rows : (part + 1) * rows, :]
    return lane_to(values, x, target)


def couplings(i, x, nx, m_scr, p_scr, m_halo, p_halo):
    m_c = m_scr[i + 1]
    p_c = p_scr[i + 1]
    m_sum = m_scr[i] + 3.0 * m_scr[i + 2] + beside_sum(m_c, *m_halo)
    p_sum = p_scr[i] + 3.0 * p_scr[i + 2] + beside_sum(p_c, *p_halo)
    kept = jnp.where(x == nx - 1, 0.8, 1.0)
    return m_c, p_c, 0.1 * m_sum, kept - 0.1 * p_sum


def halos(x, ny, part_m, y_low, y_high, z_low, z_high):
    lanes = z_low.shape[1]
    return (
        y_low[part_m, pl.ds(x, 1), :],
        y_high[part_m, pl.ds(x, 1), :],
        halo_column(z_low, part_m, ny, x, 0),
        halo_column(z_high, part_m, ny, x, lanes - 1),
    )


def faces_kernel(adj_ref, pore_ref, y_low, y_high, z_low, z_high):
    planes, ny, nz = adj_ref.shape
    nx = z_low.shape[1]
    step = pl.program_id(0)
    lane = lax.broadcasted_iota(jnp.int32, (ny, nx), 1)

    def body(i, carry):
        x = step * planes + i
        pores = pore_ref[i].astype(F32)
        out = list(carry)
        for part, value in enumerate((adj_ref[i] * pores, pores)):
            y_low[part, pl.ds(x, 1), :] = value[:1]
            y_high[part, pl.ds(x, 1), :] = value[ny - 1 :]
            out[part] = jnp.where(lane == x, lane_to(value[:, :nx], 0, x), out[part])
            out[2 + part] = jnp.where(lane == x, lane_to(value[:, nz - nx :], nx - 1, x), out[2 + part])
        return tuple(out)

    parts = [z_low[:ny], z_low[ny:], z_high[:ny], z_high[ny:]]
    parts = lax.fori_loop(0, planes, body, tuple(parts))
    z_low[:ny], z_low[ny:], z_high[:ny], z_high[ny:] = parts


def faces(adjoint, pores, planes=16):
    nx, ny, nz = adjoint.shape
    block = pl.BlockSpec((planes, ny, nz), lambda t: (t, 0, 0))
    y_spec = pl.BlockSpec((2, nx, nz), lambda t: (0, 0, 0))
    z_spec = pl.BlockSpec((2 * ny, nx), lambda t: (0, 0))
    y_shape = jax.ShapeDtypeStruct((2, nx, nz), F32)
    z_shape = jax.ShapeDtypeStruct((2 * ny, nx), F32)
    return pl.pallas_call(
        faces_kernel,
        grid=(nx // planes,),
        in_specs=[block, block],
        out_specs=[y_spec, y_spec, z_spec, z_spec],
        out_shape=[y_shape, y_shape, z_shape, z_shape],
        compiler_params=pltpu.CompilerParams(vmem_limit_bytes=VMEM_LIMIT),
        cost_estimate=pl.CostEstimate(flops=nx * ny * nz, bytes_accessed=8 * nx * ny * nz, transcendentals=0),
        name="faces",
    )(adjoint, pores)


def stage_kernel(first, count, planes, nx, split, has_prior, *refs):
    (table, which, affinities, adj, pore, cap, f_late, f_early, o_late, y_low, y_high, z_low, z_high), refs = refs[:13], refs[13:]
    prior = ()
    if has_prior:
        prior, refs = refs[1:5], refs[5:]
    next_adj, *next_faces = refs[:5]
    outs, (m_scr, p_scr) = refs[5:-2], refs[-2:]
    ny, nz = cap.shape[1:]
    step = pl.program_id(0)
    start = table[first + step]
    affinity = affinities[which[0]]
    out_y_low, out_y_high, out_z_low, out_z_high = next_faces

    if has_prior:

        @pl.when(step == 0)
        def _():
            for new, old in zip(next_faces, prior):
                new[...] = old[...]

    gather_window(start, planes, nx, adj, pore, m_scr, p_scr, False)
    lane = lax.broadcasted_iota(jnp.int32, (ny, nx), 1)

    def run(grad_ref):
        def body(i, carry):
            low, high = carry
            x = start + i
            m_halo = halos(x, ny, 0, y_low, y_high, z_low, z_high)
            p_halo = halos(x, ny, 1, y_low, y_high, z_low, z_high)
            m_c, p_c, inflow, kept = couplings(i, x, nx, m_scr, p_scr, m_halo, p_halo)
            filled = f_late[i].astype(F32)
            late = reciprocal(1.0 + affinity * filled)
            kept = kept - cap[i] * (affinity * late * late)
            updated = m_c * kept + p_c * (inflow + (filled - o_late[i].astype(F32)))
            next_adj[i] = updated
            early = reciprocal(1.0 + affinity * f_early[i].astype(F32))
            grad_ref[i] = (late - 1.0) * m_c + (early - 1.0) * updated
            out_y_low[pl.ds(x, 1), :] = updated[:1]
            out_y_high[pl.ds(x, 1), :] = updated[ny - 1 :]
            low = jnp.where(lane == x, lane_to(updated[:, :nx], 0, x), low)
            high = jnp.where(lane == x, lane_to(updated[:, nz - nx :], nx - 1, x), high)
            return low, high

        low, high = lax.fori_loop(0, planes, body, (out_z_low[...], out_z_high[...]))
        out_z_low[...] = low
        out_z_high[...] = high

    if split:
        for k, grad_ref in enumerate(outs):
            pl.when(step == k)(functools.partial(run, grad_ref))
    else:
        run(outs[0])


def stage(scalars, fields, halo, prior, first, count, planes, split, name):
    adjoint, pores, capacity, filled, seen = fields
    nx, ny, nz = adjoint.shape
    el = pl.Element
    full = (el(ny), el(nz))

    def at(moment):
        return pl.BlockSpec((el(planes), *full), lambda t, table, *_: (table[first + t] + moment * nx, 0, 0))

    wide = pl.BlockSpec((el(planes + 2), *full), lambda t, table, *_: (window(table[first + t], planes, nx), 0, 0))

    def whole(shape):
        return pl.BlockSpec(shape, lambda t, *_: (0,) * len(shape))

    face_shapes = [(nx, nz), (nx, nz), (ny, nx), (ny, nx)]
    in_specs = [wide, wide, at(0), at(1), at(0), at(1)] + [whole(h.shape) for h in halo]
    operands = [adjoint, pores, capacity, filled, filled, seen, *halo]
    aliases = {}
    if prior is not None:
        aliases = {len(scalars) + len(operands): 0}
        in_specs += [pl.BlockSpec(memory_space=pl.ANY)] + [whole(s) for s in face_shapes]
        operands += list(prior)
    out_specs = [at(0)] + [whole(s) for s in face_shapes]
    out_shape = [jax.ShapeDtypeStruct((nx, ny, nz), F32)] + [jax.ShapeDtypeStruct(s, F32) for s in face_shapes]
    if split:
        out_specs += [whole((planes, ny, nz))] * count
        out_shape += [jax.ShapeDtypeStruct((planes, ny, nz), F32)] * count
    else:
        out_specs += [pl.BlockSpec((planes, ny, nz), lambda t, *_: (t, 0, 0))]
        out_shape += [jax.ShapeDtypeStruct((count * planes, ny, nz), F32)]
    voxels = count * planes * ny * nz
    results = pl.pallas_call(
        functools.partial(stage_kernel, first, count, planes, nx, split, prior is not None),
        grid_spec=pltpu.PrefetchScalarGridSpec(
            num_scalar_prefetch=len(scalars),
            grid=(count,),
            in_specs=in_specs,
            out_specs=out_specs,
            scratch_shapes=[pltpu.VMEM((planes + 2, ny, nz), F32)] * 2,
        ),
        out_shape=out_shape,
        input_output_aliases=aliases,
        compiler_params=pltpu.CompilerParams(vmem_limit_bytes=VMEM_LIMIT),
        cost_estimate=pl.CostEstimate(flops=50 * voxels, bytes_accessed=28 * voxels, transcendentals=2 * voxels),
        name=name,
    )(*scalars, *operands)
    return results[:5], results[5:]


def last_kernel(nx, which, affinities, adj, pore, cap, f_early, o_early, m_yl, m_yh, m_zl, m_zh, y_low, y_high, z_low, z_high, out, m_scr, p_scr):
    planes, ny, _ = cap.shape
    start = pl.program_id(0) * planes
    affinity = affinities[which[0]]
    gather_window(start, planes, nx, adj, pore, m_scr, p_scr, True)

    def body(i, _):
        x = start + i
        lanes = m_zl.shape[1]
        m_halo = (
            m_yl[pl.ds(x, 1), :],
            m_yh[pl.ds(x, 1), :],
            halo_column(m_zl, 0, ny, x, 0),
            halo_column(m_zh, 0, ny, x, lanes - 1),
        )
        p_halo = halos(x, ny, 1, y_low, y_high, z_low, z_high)
        m_c, p_c, inflow, kept = couplings(i, x, nx, m_scr, p_scr, m_halo, p_halo)
        filled = f_early[i].astype(F32)
        early = reciprocal(1.0 + affinity * filled)
        kept = kept - cap[i] * (affinity * early * early)
        out[i] = m_c * kept + p_c * (inflow + (filled - o_early[i].astype(F32)))
        return 0

    lax.fori_loop(0, planes, body, 0)


def last_step(scalars, fields, halo, face_halo, planes=16):
    adjoint, pores, capacity, filled, seen = fields
    nx, ny, nz = adjoint.shape
    el = pl.Element

    block = pl.BlockSpec((planes, ny, nz), lambda t, *_: (t, 0, 0))
    wide = pl.BlockSpec((el(planes + 2), el(ny), el(nz)), lambda t, *_: (window(t * planes, planes, nx), 0, 0))

    def whole(shape):
        return pl.BlockSpec(shape, lambda t, *_: (0,) * len(shape))

    voxels = nx * ny * nz
    return pl.pallas_call(
        functools.partial(last_kernel, nx),
        grid_spec=pltpu.PrefetchScalarGridSpec(
            num_scalar_prefetch=len(scalars),
            grid=(nx // planes,),
            in_specs=[wide, wide, block, block, block] + [whole(h.shape) for h in (*face_halo, *halo)],
            out_specs=block,
            scratch_shapes=[pltpu.VMEM((planes + 2, ny, nz), F32)] * 2,
        ),
        out_shape=jax.ShapeDtypeStruct((nx, ny, nz), F32),
        compiler_params=pltpu.CompilerParams(vmem_limit_bytes=VMEM_LIMIT),
        cost_estimate=pl.CostEstimate(flops=40 * voxels, bytes_accessed=20 * voxels, transcendentals=voxels),
        name="last_step",
    )(*scalars, adjoint, pores, capacity, filled, seen, *face_halo, *halo)


def exchange(y_low, y_high, z_low, z_high):
    received = []
    for axis, low, high in (("gy", y_low, y_high), ("gz", z_low, z_high)):
        count = lax.axis_size(axis)
        up = [(i, i + 1) for i in range(count - 1)]
        down = [(i + 1, i) for i in range(count - 1)]
        received += [lax.ppermute(high, axis, up), lax.ppermute(low, axis, down)]
    return tuple(received)


def shards(ring, adjoint_final, concentration, observed, capacity, pore_mask, feed_index, feed_affinity):
    ranks = lax.axis_size("exp")
    pairs = ranks // ring
    adjoint = adjoint_final[0]
    nx, ny, nz = adjoint.shape
    share = nx // ranks
    size_p = (share * 5) // 8
    size_q = share - size_p
    filled = concentration.reshape(-1, ny, nz)
    seen = observed.reshape(-1, ny, nz)

    rank = lax.axis_index("exp")
    row, half = rank // pairs, rank % pairs

    def send(value, turn, swap):
        perm = [
            (r * pairs + h, ((r + turn) % ring) * pairs + (h + swap) % pairs) for r in range(ring) for h in range(pairs)
        ]
        return lax.ppermute(value, "exp", perm)

    def owner(turn, swap):
        return ((row + turn) % ring) * pairs + (half + swap) % pairs

    order = [(2, 1, 0), (2, 0, 0)]
    order += [(turn, 1, size_p) for turn in range(ring)]
    order += [(1, 0, 0), (3, 1, 0), (1, 1, 0), (3, 0, 0), (0, 1, 0), (0, 0, 0)]
    order += [(turn, 0, size_p) for turn in range(ring)]
    table = jnp.stack([owner(turn, swap) * share + offset for turn, swap, offset in order]).astype(jnp.int32)
    scalars = (table, feed_index, feed_affinity)

    halo = exchange(*faces(adjoint, pore_mask))
    fields = (adjoint, pore_mask, capacity, filled, seen)
    state, (far_s, far_k) = stage(scalars, fields, halo, None, 0, 2, size_p, True, "far")
    got_s, got_k = send(far_s, 1, 0), send(far_k, 3, 0)
    state, (cross,) = stage(scalars, fields, halo, state, 2, 4, size_q, False, "cross")
    crossed = send(cross, 0, 1)
    state, (up_k, dn_s, up_s, dn_k, own_s, own_k) = stage(scalars, fields, halo, state, 6, 6, size_p, True, "near")
    from_low_k, from_high_s = send(up_k, 1, 0), send(dn_s, 3, 0)
    state, (kept,) = stage(scalars, fields, halo, state, 12, 4, size_q, False, "kept")

    next_adjoint, *next_faces = state
    face_halo = exchange(*next_faces)

    from_low_s, from_high_k = send(up_s + got_s, 1, 0), send(dn_k + got_k, 3, 0)
    sums = (kept + crossed).reshape(ring, size_q, ny, nz)
    part_2, part_1, part_3 = send(sums[2], 2, 0), send(sums[1], 1, 0), send(sums[3], 3, 0)
    last_p = send(own_s + from_low_s + from_high_s, 0, 1)

    adjoint_first = last_step((feed_index, feed_affinity), (next_adjoint, pore_mask, capacity, filled, seen), halo, face_halo)

    total_p = own_k + from_low_k + from_high_k + last_p
    total_q = sums[0] + part_1 + part_2 + part_3
    return adjoint_first[None], jnp.concatenate([total_p, total_q], 0)


def solution(mesh):
    in_specs = (
        P("exp", None, "gy", "gz"),
        P(None, "exp", None, "gy", "gz"),
        P(None, "exp", None, "gy", "gz"),
        P(None, "gy", "gz"),
        P(None, "gy", "gz"),
        P("exp"),
        P(),
    )
    out_specs = (P("exp", None, "gy", "gz"), P("exp", "gy", "gz"))
    return jax.shard_map(
        functools.partial(shards, 4), mesh=mesh, in_specs=in_specs, out_specs=out_specs, check_vma=False
    )
```

```python
import functools

import jax
import jax.numpy as jnp
from jax import lax
from jax.experimental import pallas as pl
from jax.experimental.pallas import tpu as pltpu
from jax.sharding import PartitionSpec as P

F32 = jnp.float32
SOLID = float("inf")
VMEM_LIMIT = 16 * 1024 * 1024
LANES = 128
ROWS = 8
VMEM = pl.BlockSpec(memory_space=pltpu.VMEM)
SMEM = pl.BlockSpec(memory_space=pltpu.SMEM)
HBM = pl.BlockSpec(memory_space=pltpu.HBM)


def reciprocal(value):
    guess = pl.reciprocal(value, approx=True)
    return guess * (2.0 - value * guess)


def lane_to(values, source, target):
    shift = target - source
    if isinstance(shift, int):
        return pltpu.roll(values, shift % LANES, 1)
    return pltpu.roll(values, lax.rem(shift + LANES, LANES), 1)


def in_hbm(*arrays):
    return [pltpu.with_memory_space_constraint(a, pltpu.HBM) for a in arrays]


def in_vmem(*arrays):
    return [pltpu.with_memory_space_constraint(a, pltpu.VMEM) for a in arrays]


def over(planes, unroll, body, carry=()):
    def some(k, carry):
        for u in range(unroll):
            carry = body(k * unroll + u, carry)
        return carry

    return lax.fori_loop(0, planes // unroll, some, carry)


def run(h):
    return slice(h * LANES, (h + 1) * LANES)


def padded_shape(nx, ny, nz):
    return (nz // LANES, nx + 2, ny + 2 * ROWS, LANES)


def halo_rows(wide, x, low, high):
    ny = wide.shape[2] - 2 * ROWS
    for h in range(wide.shape[0]):
        wide[h, x + 1, ROWS - 1 : ROWS, :] = low[:, run(h)]
        wide[h, x + 1, ROWS + ny : ROWS + ny + 1, :] = high[:, run(h)]


def weighted(wide, at, lane, z_low, z_high):
    count, _, rows, _ = wide.shape
    ny = rows - 2 * ROWS
    inner = slice(ROWS, ROWS + ny)
    centre = [wide[h, at, inner, :] for h in range(count)]
    ups = [pltpu.roll(c, 1, 1) for c in centre]
    downs = [pltpu.roll(c, LANES - 1, 1) for c in centre]
    sums = []
    for h in range(count):
        total = wide[h, at, ROWS - 1 : ROWS - 1 + ny, :] + wide[h, at, ROWS + 1 : ROWS + 1 + ny, :]
        total = total + (wide[h, at - 1, inner, :] + 3.0 * wide[h, at + 1, inner, :])
        left = jnp.where(lane == 0, ups[h - 1] if h else z_low, ups[h])
        right = jnp.where(lane == LANES - 1, downs[h + 1] if h + 1 < count else z_high, downs[h])
        sums.append(total + (left + right))
    return centre, sums


def rotating(steps, copies, body):
    for copy in copies(0, 0):
        copy.start()
    for t in range(steps):
        slot = t % 2
        if t + 1 < steps:
            for copy in copies(t + 1, 1 - slot):
                copy.start()
        for copy in copies(t, slot):
            copy.wait()
        body(t, slot)


def prepare_kernel(planes, unroll, adj_hbm, pore_hbm, masked, kept, y_low, y_high, z_low, z_high, adj, pore, wide, sem):
    nx, ny, nz = adj_hbm.shape
    count = nz // LANES
    lane = lax.broadcasted_iota(jnp.int32, (ny, LANES), 1)
    steps = nx // planes

    for h in range(count):
        for x in (0, nx + 1):
            masked[h, x] = jnp.zeros_like(masked[h, x])
            wide[h, x] = jnp.zeros_like(wide[h, x])

    def clear(x, carry):
        for h in range(count):
            wide[h, x + 1, :ROWS, :] = jnp.zeros((ROWS, LANES), F32)
            wide[h, x + 1, ROWS + ny :, :] = jnp.zeros((ROWS, LANES), F32)
        return carry

    def copies(t, slot):
        at = pl.ds(t * planes, planes)
        return [
            pltpu.make_async_copy(adj_hbm.at[at], adj.at[slot], sem.at[slot, 0]),
            pltpu.make_async_copy(pore_hbm.at[at], pore.at[slot], sem.at[slot, 1]),
        ]

    def body(t, slot):
        def load(i, carry):
            x = t * planes + i
            here = lane == x
            out = list(carry)
            clear(x, ())
            pores = pore[slot, i].astype(F32)
            for part, value in enumerate((adj[slot, i] * pores, pores)):
                halves = [value[:, run(h)] for h in range(count)]
                for h in range(count):
                    (wide if part else masked)[h, x + 1, ROWS : ROWS + ny, :] = halves[h]
                y_low[part, pl.ds(x, 1), :] = value[:1]
                y_high[part, pl.ds(x, 1), :] = value[ny - 1 :]
                out[part] = jnp.where(here, lane_to(halves[0], 0, x), out[part])
                out[2 + part] = jnp.where(here, lane_to(halves[-1], LANES - 1, x), out[2 + part])
            return tuple(out)

        parts = (z_low[:ny], z_low[ny:], z_high[:ny], z_high[ny:])
        z_low[:ny], z_low[ny:], z_high[:ny], z_high[ny:] = over(planes, unroll, load, parts)

        def weigh(i, carry):
            x = t * planes + i - 1 if t else i
            zero = jnp.zeros((ny, LANES), F32)
            pores, sums = weighted(wide, x + 1, lane, zero, zero)
            outer = jnp.where(x == nx - 1, 0.8, 1.0)
            for h in range(count):
                kept[h, x] = jnp.where(pores[h] > 0.0, outer - 0.1 * sums[h], SOLID)
            return carry

        over(planes if t else planes - 1, unroll if t else 1, weigh)
        if t == steps - 1:
            weigh(planes, ())

    rotating(steps, copies, body)


def prepare(adjoint, pores, planes=16, unroll=4):
    nx, ny, nz = adjoint.shape
    y_shape = jax.ShapeDtypeStruct((2, nx, nz), F32)
    z_shape = jax.ShapeDtypeStruct((2 * ny, nx), F32)
    wide = padded_shape(nx, ny, nz)
    return pl.pallas_call(
        functools.partial(prepare_kernel, planes, unroll),
        in_specs=[HBM, HBM],
        out_specs=[VMEM] * 6,
        out_shape=[
            pltpu.VMEM(wide, F32),
            pltpu.VMEM((nz // LANES, nx, ny, LANES), F32),
            y_shape,
            y_shape,
            z_shape,
            z_shape,
        ],
        scratch_shapes=[
            pltpu.VMEM((2, planes, ny, nz), F32),
            pltpu.VMEM((2, planes, ny, nz), jnp.int32),
            pltpu.VMEM(wide, F32),
            pltpu.SemaphoreType.DMA((2, 2)),
        ],
        compiler_params=pltpu.CompilerParams(vmem_limit_bytes=VMEM_LIMIT),
        cost_estimate=pl.CostEstimate(flops=14 * nx * ny * nz, bytes_accessed=8 * nx * ny * nz, transcendentals=0),
        name="prepare",
    )(*in_hbm(adjoint, pores))


def stage_kernel(places, counts, planes, unroll, fresh, *refs):
    which, affinities, cap_hbm, filled_hbm, seen_hbm, y_low, y_high, z_low, z_high = refs[:9]
    refs = refs[9 + (2 if fresh else 7) :]
    (masked, kept, adj, out_y_low, out_y_high, out_z_low, out_z_high), refs = refs[:7], refs[7:]
    outs, (cap, late_f, early_f, late_o, sem) = refs[:-5], refs[-5:]
    count, nx, ny, _ = kept.shape
    lane = lax.broadcasted_iota(jnp.int32, (ny, LANES), 1)
    starts = places()
    inverse = 1.0 / jnp.full((1, LANES), affinities[which[0]], F32)

    if fresh:
        for h in range(count):
            for x in (0, nx + 1):
                adj[h, x] = jnp.zeros_like(adj[h, x])

    def copies(t, slot):
        start = starts[t]
        pairs = [
            (cap_hbm, start, cap),
            (filled_hbm, start + nx, late_f),
            (filled_hbm, start, early_f),
            (seen_hbm, start + nx, late_o),
        ]
        return [
            pltpu.make_async_copy(src.at[pl.ds(at, planes)], dst.at[slot], sem.at[slot, k])
            for k, (src, at, dst) in enumerate(pairs)
        ]

    targets = [(out, k) for out, n in zip(outs, counts) for k in range(n)]

    def body(t, slot):
        start = starts[t]
        grad, block = targets[t]
        m_low, p_low = z_low[:ny], 0.1 * z_low[ny:]
        m_high, p_high = z_high[:ny], 0.1 * z_high[ny:]

        def ends(i, carry):
            x = start + i
            row = pl.ds(x, 1)
            halo_rows(masked, x, y_low[0, row, :], y_high[0, row, :])
            low, high = 0.1 * y_low[1, row, :], 0.1 * y_high[1, row, :]
            for h in range(count):
                kept[h, x, :1, :] = kept[h, x, :1, :] - low[:, run(h)]
                kept[h, x, ny - 1 :, :] = kept[h, x, ny - 1 :, :] - high[:, run(h)]
            return carry

        over(planes, unroll, ends)

        def plane(i, carry):
            low, high = carry
            x = start + i
            m_c, m_sum = weighted(masked, x + 1, lane, lane_to(m_low, x, 0), lane_to(m_high, x, LANES - 1))
            values = []
            for h in range(count):
                filled = late_f[slot, i, :, run(h)].astype(F32)
                early = early_f[slot, i, :, run(h)].astype(F32)
                source = filled - late_o[slot, i, :, run(h)].astype(F32)
                late_r = reciprocal(-inverse - filled)
                early_r = reciprocal(-inverse - early)
                weight = kept[h, x]
                if h == 0:
                    weight = weight - jnp.where(lane == 0, lane_to(p_low, x, 0), 0.0)
                if h == count - 1:
                    weight = weight - jnp.where(lane == LANES - 1, lane_to(p_high, x, LANES - 1), 0.0)
                pore = weight != SOLID
                uptake = cap[slot, i, :, run(h)] * inverse
                updated = m_c[h] * (weight - uptake * (late_r * late_r)) + (0.1 * m_sum[h] + source)
                updated = jnp.where(pore, updated, 0.0)
                kept[h, x] = jnp.where(pore, weight - uptake * (early_r * early_r), SOLID)
                grad[block * planes + i, :, run(h)] = (filled * late_r) * m_c[h] + (early * early_r) * updated
                adj[h, x + 1, ROWS : ROWS + ny, :] = updated
                values.append(updated)
            out_y_low[pl.ds(x, 1), :] = jnp.concatenate([v[:1] for v in values], 1)
            out_y_high[pl.ds(x, 1), :] = jnp.concatenate([v[ny - 1 :] for v in values], 1)
            low = jnp.where(lane == x, lane_to(values[0], 0, x), low)
            high = jnp.where(lane == x, lane_to(values[-1], LANES - 1, x), high)
            return low, high

        out_z_low[...], out_z_high[...] = over(planes, unroll, plane, (out_z_low[...], out_z_high[...]))

    rotating(sum(counts), copies, body)


def stage(scalars, fields, halo, state, places, counts, planes, unroll, name):
    capacity, filled, seen = fields
    nx, ny, nz = capacity.shape
    runs = sum(counts)
    operands = [*scalars, *in_hbm(capacity, filled, seen), *halo, *in_vmem(*state)]
    base = len(operands) - len(state)
    shapes = [padded_shape(nx, ny, nz), (nz // LANES, nx, ny, LANES), padded_shape(nx, ny, nz), (nx, nz), (nx, nz), (ny, nx), (ny, nx)]
    shapes += [(n * planes, ny, nz) for n in counts]
    block = (2, planes, ny, nz)
    voxels = runs * planes * ny * nz
    results = pl.pallas_call(
        functools.partial(stage_kernel, places, counts, planes, unroll, len(state) == 2),
        in_specs=[SMEM] * 2 + [HBM] * 3 + [VMEM] * (4 + len(state)),
        out_specs=[VMEM] * len(shapes),
        out_shape=[pltpu.VMEM(s, F32) for s in shapes[:7]] + [jax.ShapeDtypeStruct(s, F32) for s in shapes[7:]],
        scratch_shapes=[
            pltpu.VMEM(block, F32),
            pltpu.VMEM(block, jnp.bfloat16),
            pltpu.VMEM(block, jnp.bfloat16),
            pltpu.VMEM(block, jnp.bfloat16),
            pltpu.SemaphoreType.DMA((2, 4)),
        ],
        input_output_aliases={base + k: k for k in range(len(state))},
        compiler_params=pltpu.CompilerParams(vmem_limit_bytes=VMEM_LIMIT),
        cost_estimate=pl.CostEstimate(flops=40 * voxels, bytes_accessed=10 * voxels, transcendentals=2 * voxels),
        name=name,
    )(*operands)
    return results[:7], results[7:]


def last_kernel(planes, unroll, f_hbm, o_hbm, kept, y_low, y_high, z_low, z_high, _, out_hbm, adj, filled, seen, out, sem, out_sem):
    count, nx, ny, _ = kept.shape
    lane = lax.broadcasted_iota(jnp.int32, (ny, LANES), 1)
    steps = nx // planes

    def copies(t, slot):
        at = pl.ds(t * planes, planes)
        return [
            pltpu.make_async_copy(f_hbm.at[at], filled.at[slot], sem.at[slot, 0]),
            pltpu.make_async_copy(o_hbm.at[at], seen.at[slot], sem.at[slot, 1]),
        ]

    def writing(t):
        return pltpu.make_async_copy(out.at[t % 2], out_hbm.at[pl.ds(t * planes, planes)], out_sem.at[t % 2])

    def body(t, slot):
        if t >= 2:
            writing(t - 2).wait()

        def ends(i, carry):
            x = t * planes + i
            row = pl.ds(x, 1)
            halo_rows(adj, x, y_low[row, :], y_high[row, :])
            return carry

        over(planes, unroll, ends)

        def plane(i, carry):
            x = t * planes + i
            centre, sums = weighted(adj, x + 1, lane, lane_to(z_low[...], x, 0), lane_to(z_high[...], x, LANES - 1))
            for h in range(count):
                weight = kept[h, x]
                source = filled[slot, i, :, run(h)].astype(F32) - seen[slot, i, :, run(h)].astype(F32)
                value = centre[h] * weight + (0.1 * sums[h] + source)
                out[slot, i, :, run(h)] = jnp.where(weight == SOLID, 0.0, value)
            return carry

        over(planes, unroll, plane)
        writing(t).start()

    rotating(steps, copies, body)
    writing(steps - 2).wait()
    writing(steps - 1).wait()


def last_step(adjoint, kept, filled, seen, halo, planes=16, unroll=4):
    count, nx, ny, lanes = kept.shape
    nz = count * lanes
    voxels = nx * ny * nz
    return pl.pallas_call(
        functools.partial(last_kernel, planes, unroll),
        in_specs=[HBM, HBM] + [VMEM] * 6,
        out_specs=[HBM, VMEM],
        out_shape=[jax.ShapeDtypeStruct((nx, ny, nz), F32), pltpu.VMEM(adjoint.shape, F32)],
        scratch_shapes=[
            pltpu.VMEM((2, planes, ny, nz), jnp.bfloat16),
            pltpu.VMEM((2, planes, ny, nz), jnp.bfloat16),
            pltpu.VMEM((2, planes, ny, nz), F32),
            pltpu.SemaphoreType.DMA((2, 2)),
            pltpu.SemaphoreType.DMA((2,)),
        ],
        input_output_aliases={7: 1},
        compiler_params=pltpu.CompilerParams(vmem_limit_bytes=VMEM_LIMIT),
        cost_estimate=pl.CostEstimate(flops=20 * voxels, bytes_accessed=8 * voxels, transcendentals=0),
        name="last_step",
    )(*in_hbm(filled, seen), *in_vmem(kept), *halo, *in_vmem(adjoint))[0]


def exchange(y_low, y_high, z_low, z_high):
    received = []
    for axis, low, high in (("gy", y_low, y_high), ("gz", z_low, z_high)):
        count = lax.axis_size(axis)
        up = [(i, i + 1) for i in range(count - 1)]
        down = [(i + 1, i) for i in range(count - 1)]
        received += [lax.ppermute(high, axis, up), lax.ppermute(low, axis, down)]
    return tuple(received)


def places(ring, pairs, share, order):
    rank = lax.axis_index("exp")
    row, half = rank // pairs, rank % pairs
    return [
        (((row + turn) % ring) * pairs + (half + swap) % pairs) * share + part * (share // 2)
        for turn, swap, part in order
    ]


def orders(ring):
    cross = [(turn, 1, 1) for turn in range(ring)]
    along = [(turn, swap, 0) for turn in (2, 1, 3) for swap in (1, 0)]
    own = [(0, 1, 0), (0, 0, 0)] + [(turn, 0, 1) for turn in range(ring)]
    return cross, along, own


def shards(ring, adjoint_final, concentration, observed, capacity, pore_mask, feed_index, feed_affinity):
    ranks = lax.axis_size("exp")
    pairs = ranks // ring
    adjoint = adjoint_final[0]
    nx, ny, nz = adjoint.shape
    share = nx // ranks
    planes = share // 2
    filled = concentration.reshape(-1, ny, nz)
    seen = observed.reshape(-1, ny, nz)

    def send(value, turn, swap):
        perm = [
            (r * pairs + h, ((r + turn) % ring) * pairs + (h + swap) % pairs) for r in range(ring) for h in range(pairs)
        ]
        return lax.ppermute(value, "exp", perm)

    scalars = (feed_index, feed_affinity)
    at = [functools.partial(places, ring, pairs, share, order) for order in orders(ring)]
    fields = (capacity, filled, seen)

    *state, y_low, y_high, z_low, z_high = prepare(adjoint, pore_mask)
    halo = exchange(y_low, y_high, z_low, z_high)
    state, (cross,) = stage(scalars, fields, halo, state, at[0], (4,), planes, 2, "cross")
    crossed = send(cross, 0, 1)
    state, along = stage(scalars, fields, halo, state, at[1], (2, 2, 2), planes, 2, "along")
    parts_p = [send(value, turn, 0) for value, turn in zip(along, (2, 1, 3))]
    (_, kept, next_adjoint, *next_faces), (own_p, own_q) = stage(scalars, fields, halo, state, at[2], (2, 4), planes, 2, "own")
    face_halo = exchange(*next_faces)

    total_p = own_p + parts_p[0] + parts_p[1] + parts_p[2]
    last_p = send(total_p[:planes], 0, 1)
    total_q = (own_q + crossed).reshape(ring, planes, ny, nz)
    parts_q = [send(total_q[turn], turn, 0) for turn in (2, 1, 3)]

    adjoint_first = last_step(next_adjoint, kept, filled, seen, face_halo)

    sum_p = total_p[planes:] + last_p
    sum_q = total_q[0] + parts_q[0] + parts_q[1] + parts_q[2]
    return adjoint_first[None], jnp.concatenate([sum_p, sum_q], 0)


def solution(mesh):
    in_specs = (
        P("exp", None, "gy", "gz"),
        P(None, "exp", None, "gy", "gz"),
        P(None, "exp", None, "gy", "gz"),
        P(None, "gy", "gz"),
        P(None, "gy", "gz"),
        P("exp"),
        P(),
    )
    out_specs = (P("exp", None, "gy", "gz"), P("exp", "gy", "gz"))
    return jax.shard_map(
        functools.partial(shards, 4), mesh=mesh, in_specs=in_specs, out_specs=out_specs, check_vma=False
    )
```

```python
import functools

import jax
import jax.numpy as jnp
from jax import lax
from jax.experimental import pallas as pl
from jax.experimental.pallas import tpu as pltpu
from jax.sharding import PartitionSpec as P

F32 = jnp.float32
SOLID = float("inf")
VMEM_LIMIT = 16 * 1024 * 1024
LANES = 128
ROWS = 8
UNROLL = (8, 4)
VMEM = pl.BlockSpec(memory_space=pltpu.VMEM)
ANY = pl.BlockSpec(memory_space=pl.ANY)
SMEM = pl.BlockSpec(memory_space=pltpu.SMEM)
HBM = pl.BlockSpec(memory_space=pltpu.HBM)


def lane_to(values, source, target):
    shift = target - source
    if isinstance(shift, int):
        return pltpu.roll(values, shift % LANES, 1)
    return pltpu.roll(values, lax.rem(shift + LANES, LANES), 1)


def in_hbm(*arrays):
    return [pltpu.with_memory_space_constraint(a, pltpu.HBM) for a in arrays]


def in_vmem(*arrays):
    return [pltpu.with_memory_space_constraint(a, pltpu.VMEM) for a in arrays]


def over(planes, unroll, body, carry=()):
    def some(k, carry):
        stores = []
        for u in range(unroll):
            carry, more = body(k * unroll + u, carry)
            stores += more
        for ref, index, value in stores:
            ref[index] = value
        return carry

    if unroll == planes:
        return some(0, carry)
    return lax.fori_loop(0, planes // unroll, some, carry)


def run(h):
    return slice(h * LANES, (h + 1) * LANES)


def padded_shape(nx, ny, nz):
    return (nz // LANES, nx + 2, ny + 2 * ROWS, LANES)


def halo_rows(wide, x, low, high):
    ny = wide.shape[2] - 2 * ROWS
    stores = []
    for h in range(wide.shape[0]):
        stores.append((wide, (h, x + 1, slice(ROWS - 1, ROWS)), low[:, run(h)]))
        stores.append((wide, (h, x + 1, slice(ROWS + ny, ROWS + ny + 1)), high[:, run(h)]))
    return stores


def face_rows(wide, x, row):
    count, planes, rows, _ = wide.shape
    flat = wide.reshape(count, planes * rows, LANES)
    return [flat[h, pl.ds((x + 1) * rows + ROWS + row, ROWS, stride=rows), :] for h in range(count)]


def store_rows(face, x, values, *lead):
    at = pl.ds(pl.multiple_of(x, ROWS), ROWS)
    for h, value in enumerate(values):
        face[(*lead, at, run(h))] = value


def weighted(wide, at, lane, z_low, z_high):
    count, _, rows, _ = wide.shape
    ny = rows - 2 * ROWS
    inner = slice(ROWS, ROWS + ny)
    centre = [wide[h, at, inner, :] for h in range(count)]
    ups = [pltpu.roll(c, 1, 1) for c in centre]
    downs = [pltpu.roll(c, LANES - 1, 1) for c in centre]
    sums = []
    for h in range(count):
        total = wide[h, at, ROWS - 1 : ROWS - 1 + ny, :] + wide[h, at, ROWS + 1 : ROWS + 1 + ny, :]
        total = total + (wide[h, at - 1, inner, :] + 3.0 * wide[h, at + 1, inner, :])
        left = jnp.where(lane == 0, ups[h - 1] if h else z_low, ups[h])
        right = jnp.where(lane == LANES - 1, downs[h + 1] if h + 1 < count else z_high, downs[h])
        sums.append(total + (left + right))
    return centre, sums


def rotating(steps, copies, body):
    for copy in copies(0, 0):
        copy.start()
    for t in range(steps):
        slot = t % 2
        if t + 1 < steps:
            for copy in copies(t + 1, 1 - slot):
                copy.start()
        for copy in copies(t, slot):
            copy.wait()
        body(t, slot)


def faces_kernel(planes, unroll, adj_hbm, pore_hbm, masked, wide, y_low, y_high, z_low, z_high, adj, pore, sem):
    nx, ny, nz = adj_hbm.shape
    count = nz // LANES
    lane = lax.broadcasted_iota(jnp.int32, (ny, LANES), 1)
    steps = nx // planes

    for h in range(count):
        for x in (0, nx + 1):
            masked[h, x] = jnp.zeros_like(masked[h, x])
            wide[h, x] = jnp.zeros_like(wide[h, x])

    def copies(t, slot):
        at = pl.ds(t * planes, planes)
        return [
            pltpu.make_async_copy(adj_hbm.at[at], adj.at[slot], sem.at[slot, 0]),
            pltpu.make_async_copy(pore_hbm.at[at], pore.at[slot], sem.at[slot, 1]),
        ]

    def body(t, slot):
        def load(i, carry):
            x = t * planes + i
            here = lane == x
            out = list(carry)
            stores = []
            for h in range(count):
                pores = pore[slot, i, :, run(h)].astype(F32)
                for part, (array, value) in enumerate(((masked, adj[slot, i, :, run(h)] * pores), (wide, pores))):
                    stores.append((array, (h, x + 1, slice(ROWS, ROWS + ny)), value))
                    if h == 0:
                        out[part] = jnp.where(here, lane_to(value, 0, x), out[part])
                    if h == count - 1:
                        out[2 + part] = jnp.where(here, lane_to(value, LANES - 1, x), out[2 + part])
                for rows in (slice(0, ROWS), slice(ROWS + ny, 2 * ROWS + ny)):
                    stores.append((wide, (h, x + 1, rows), jnp.zeros((ROWS, LANES), F32)))
            return tuple(out), stores

        parts = (z_low[:ny], z_low[ny:], z_high[:ny], z_high[ny:])
        z_low[:ny], z_low[ny:], z_high[:ny], z_high[ny:] = over(planes, unroll, load, parts)

        for x in range(t * planes, (t + 1) * planes, ROWS):
            for part, array in enumerate((masked, wide)):
                store_rows(y_low, x, face_rows(array, x, 0), part)
                store_rows(y_high, x, face_rows(array, x, ny - 1), part)

    rotating(steps, copies, body)


def faces(adjoint, pores, planes=16, unroll=16):
    nx, ny, nz = adjoint.shape
    y_shape = jax.ShapeDtypeStruct((2, nx, nz), F32)
    z_shape = jax.ShapeDtypeStruct((2 * ny, nx), F32)
    wide = padded_shape(nx, ny, nz)
    return pl.pallas_call(
        functools.partial(faces_kernel, planes, unroll),
        in_specs=[HBM, HBM],
        out_specs=[VMEM] * 6,
        out_shape=[pltpu.VMEM(wide, F32), pltpu.VMEM(wide, F32), y_shape, y_shape, z_shape, z_shape],
        scratch_shapes=[
            pltpu.VMEM((2, planes, ny, nz), F32),
            pltpu.VMEM((2, planes, ny, nz), jnp.int32),
            pltpu.SemaphoreType.DMA((2, 2)),
        ],
        compiler_params=pltpu.CompilerParams(vmem_limit_bytes=VMEM_LIMIT),
        cost_estimate=pl.CostEstimate(flops=4 * nx * ny * nz, bytes_accessed=8 * nx * ny * nz, transcendentals=0),
        name="faces",
    )(*in_hbm(adjoint, pores))


def weigh_kernel(unroll, wide, kept):
    count, nx, ny, _ = kept.shape
    lane = lax.broadcasted_iota(jnp.int32, (ny, LANES), 1)
    zero = jnp.zeros((ny, LANES), F32)

    def body(x, carry):
        pores, sums = weighted(wide, x + 1, lane, zero, zero)
        outer = jnp.where(x == nx - 1, 0.8, 1.0)
        return carry, [
            (kept, (h, x), jnp.where(pores[h] > 0.0, outer - 0.1 * sums[h], SOLID)) for h in range(count)
        ]

    over(nx, unroll, body)


def weigh(wide, unroll=32):
    count, nx, rows, lanes = wide.shape
    shape = (count, nx - 2, rows - 2 * ROWS, lanes)
    voxels = shape[0] * shape[1] * shape[2] * shape[3]
    return pl.pallas_call(
        functools.partial(weigh_kernel, unroll),
        in_specs=[VMEM],
        out_specs=VMEM,
        out_shape=pltpu.VMEM(shape, F32),
        compiler_params=pltpu.CompilerParams(vmem_limit_bytes=VMEM_LIMIT),
        cost_estimate=pl.CostEstimate(flops=12 * voxels, bytes_accessed=12 * voxels, transcendentals=0),
        name="weigh",
    )(*in_vmem(wide))


def stage_kernel(places, counts, planes, unroll, fresh, *refs):
    which, affinities, cap_hbm, filled_hbm, seen_hbm, y_low, y_high, z_low, z_high = refs[:9]
    refs = refs[9 + (2 if fresh else 7) :]
    (masked, kept, adj, out_y_low, out_y_high, out_z_low, out_z_high), refs = refs[:7], refs[7:]
    outs, (cap, late_f, early_f, late_o, inflow, sem) = refs[:-6], refs[-6:]
    count, nx, ny, _ = kept.shape
    lane = lax.broadcasted_iota(jnp.int32, (ny, LANES), 1)
    starts = places()
    inverse = 1.0 / jnp.full((1, LANES), affinities[which[0]], F32)

    if fresh:
        for h in range(count):
            for x in (0, nx + 1):
                adj[h, x] = jnp.zeros_like(adj[h, x])

    def copies(t, slot):
        start = starts[t]
        pairs = [
            (cap_hbm, start, cap),
            (filled_hbm, start + nx, late_f),
            (filled_hbm, start, early_f),
            (seen_hbm, start + nx, late_o),
        ]
        return [
            pltpu.make_async_copy(src.at[pl.ds(at, planes)], dst.at[slot], sem.at[slot, k])
            for k, (src, at, dst) in enumerate(pairs)
        ]

    targets = [(out, k) for out, n in zip(outs, counts) for k in range(n)]

    def body(t, slot):
        start = starts[t]
        grad, block = targets[t]
        m_low, p_low = z_low[:ny], 0.1 * z_low[ny:]
        m_high, p_high = z_high[:ny], 0.1 * z_high[ny:]

        def ends(i, carry):
            x = start + i
            row = pl.ds(x, 1)
            stores = halo_rows(masked, x, y_low[0, row, :], y_high[0, row, :])
            low, high = 0.1 * y_low[1, row, :], 0.1 * y_high[1, row, :]
            for h in range(count):
                for rows, value in ((slice(0, 1), low), (slice(ny - 1, ny), high)):
                    stores.append((kept, (h, x, rows), kept[h, x, rows, :] - value[:, run(h)]))
            return carry, stores

        over(planes, planes, ends)

        def gather(i, carry):
            x = start + i
            _, sums = weighted(masked, x + 1, lane, lane_to(m_low, x, 0), lane_to(m_high, x, LANES - 1))
            return carry, [(inflow, (h, i), 0.1 * sums[h]) for h in range(count)]

        over(planes, unroll[0], gather)

        def plane(i, carry):
            low, high = carry
            x = start + i
            stores = []
            for h in range(count):
                centre = masked[h, x + 1, ROWS : ROWS + ny, :]
                filled = late_f[slot, i, :, run(h)].astype(F32)
                early = early_f[slot, i, :, run(h)].astype(F32)
                source = filled - late_o[slot, i, :, run(h)].astype(F32)
                late_r = pl.reciprocal(-inverse - filled, approx=True)
                early_r = pl.reciprocal(-inverse - early, approx=True)
                weight = kept[h, x]
                if h == 0:
                    weight = weight - jnp.where(lane == 0, lane_to(p_low, x, 0), 0.0)
                if h == count - 1:
                    weight = weight - jnp.where(lane == LANES - 1, lane_to(p_high, x, LANES - 1), 0.0)
                pore = weight != SOLID
                uptake = cap[slot, i, :, run(h)] * inverse
                updated = centre * (weight - uptake * (late_r * late_r)) + (inflow[h, i] + source)
                updated = jnp.where(pore, updated, 0.0)
                stores.append((kept, (h, x), jnp.where(pore, weight - uptake * (early_r * early_r), SOLID)))
                term = (filled * late_r) * centre + (early * early_r) * updated
                stores.append((grad, (block * planes + i, slice(None), run(h)), term))
                stores.append((adj, (h, x + 1, slice(ROWS, ROWS + ny)), updated))
                if h == 0:
                    low = jnp.where(lane == x, lane_to(updated, 0, x), low)
                if h == count - 1:
                    high = jnp.where(lane == x, lane_to(updated, LANES - 1, x), high)
            return (low, high), stores

        out_z_low[...], out_z_high[...] = over(planes, unroll[1], plane, (out_z_low[...], out_z_high[...]))
        for at in range(0, planes, ROWS):
            store_rows(out_y_low, start + at, face_rows(adj, start + at, 0))
            store_rows(out_y_high, start + at, face_rows(adj, start + at, ny - 1))

    rotating(sum(counts), copies, body)


def stage(scalars, fields, halo, state, places, counts, planes, unroll, name):
    capacity, filled, seen = fields
    nx, ny, nz = capacity.shape
    runs = sum(counts)
    operands = [*scalars, *in_hbm(capacity, filled, seen), *halo, *in_vmem(*state)]
    base = len(operands) - len(state)
    shapes = [padded_shape(nx, ny, nz), (nz // LANES, nx, ny, LANES), padded_shape(nx, ny, nz), (nx, nz), (nx, nz), (ny, nx), (ny, nx)]
    shapes += [(n * planes, ny, nz) for n in counts]
    block = (2, planes, ny, nz)
    voxels = runs * planes * ny * nz
    results = pl.pallas_call(
        functools.partial(stage_kernel, places, counts, planes, unroll, len(state) == 2),
        in_specs=[SMEM] * 2 + [HBM] * 3 + [VMEM] * (4 + len(state)),
        out_specs=[VMEM] * len(shapes),
        out_shape=[pltpu.VMEM(s, F32) for s in shapes[:7]] + [jax.ShapeDtypeStruct(s, F32) for s in shapes[7:]],
        scratch_shapes=[
            pltpu.VMEM(block, F32),
            pltpu.VMEM(block, jnp.bfloat16),
            pltpu.VMEM(block, jnp.bfloat16),
            pltpu.VMEM(block, jnp.bfloat16),
            pltpu.VMEM((nz // LANES, planes, ny, LANES), F32),
            pltpu.SemaphoreType.DMA((2, 4)),
        ],
        input_output_aliases={base + k: k for k in range(len(state))},
        compiler_params=pltpu.CompilerParams(vmem_limit_bytes=VMEM_LIMIT),
        cost_estimate=pl.CostEstimate(flops=40 * voxels, bytes_accessed=10 * voxels, transcendentals=2 * voxels),
        name=name,
    )(*operands)
    return results[:7], results[7:]


def last_kernel(planes, unroll, f_hbm, o_hbm, kept, y_low, y_high, z_low, z_high, _, _after, out_hbm, adj, filled, seen, out, sem, out_sem):
    count, nx, ny, _ = kept.shape
    lane = lax.broadcasted_iota(jnp.int32, (ny, LANES), 1)
    steps = nx // planes

    def copies(t, slot):
        at = pl.ds(t * planes, planes)
        return [
            pltpu.make_async_copy(f_hbm.at[at], filled.at[slot], sem.at[slot, 0]),
            pltpu.make_async_copy(o_hbm.at[at], seen.at[slot], sem.at[slot, 1]),
        ]

    def writing(t):
        return pltpu.make_async_copy(out.at[t % 2], out_hbm.at[pl.ds(t * planes, planes)], out_sem.at[t % 2])

    def body(t, slot):
        if t >= 2:
            writing(t - 2).wait()

        def ends(i, carry):
            x = t * planes + i
            row = pl.ds(x, 1)
            return carry, halo_rows(adj, x, y_low[row, :], y_high[row, :])

        over(planes, planes, ends)

        def plane(i, carry):
            x = t * planes + i
            centre, sums = weighted(adj, x + 1, lane, lane_to(z_low[...], x, 0), lane_to(z_high[...], x, LANES - 1))
            stores = []
            for h in range(count):
                weight = kept[h, x]
                source = filled[slot, i, :, run(h)].astype(F32) - seen[slot, i, :, run(h)].astype(F32)
                value = centre[h] * weight + (0.1 * sums[h] + source)
                stores.append((out, (slot, i, slice(None), run(h)), jnp.where(weight == SOLID, 0.0, value)))
            return carry, stores

        over(planes, unroll, plane)
        writing(t).start()

    rotating(steps, copies, body)
    writing(steps - 2).wait()
    writing(steps - 1).wait()


def last_step(adjoint, kept, filled, seen, halo, after, planes=16, unroll=16):
    count, nx, ny, lanes = kept.shape
    nz = count * lanes
    voxels = nx * ny * nz
    return pl.pallas_call(
        functools.partial(last_kernel, planes, unroll),
        in_specs=[HBM, HBM] + [VMEM] * 6 + [ANY],
        out_specs=[HBM, VMEM],
        out_shape=[jax.ShapeDtypeStruct((nx, ny, nz), F32), pltpu.VMEM(adjoint.shape, F32)],
        scratch_shapes=[
            pltpu.VMEM((2, planes, ny, nz), jnp.bfloat16),
            pltpu.VMEM((2, planes, ny, nz), jnp.bfloat16),
            pltpu.VMEM((2, planes, ny, nz), F32),
            pltpu.SemaphoreType.DMA((2, 2)),
            pltpu.SemaphoreType.DMA((2,)),
        ],
        input_output_aliases={7: 1},
        compiler_params=pltpu.CompilerParams(vmem_limit_bytes=VMEM_LIMIT),
        cost_estimate=pl.CostEstimate(flops=20 * voxels, bytes_accessed=8 * voxels, transcendentals=0),
        name="last_step",
    )(*in_hbm(filled, seen), *in_vmem(kept), *halo, *in_vmem(adjoint), after)[0]


def add_kernel(n_parts, n_after, unroll, *refs):
    parts, outs = refs[:n_parts], refs[n_parts + n_after :]
    planes = outs[0].shape[0]

    def body(i, carry):
        stores = []
        for k, out in enumerate(outs):
            total = parts[0][k * planes + i]
            for part in parts[1:]:
                total = total + part[k * planes + i]
            stores.append((out, (i,), total))
        return carry, stores

    over(planes, unroll, body)


def add(parts, after, pieces, name, unroll=2):
    planes, ny, nz = parts[0].shape
    shape = jax.ShapeDtypeStruct((planes // pieces, ny, nz), F32)
    size = planes * ny * nz
    return pl.pallas_call(
        functools.partial(add_kernel, len(parts), len(after), unroll),
        in_specs=[VMEM] * len(parts) + [ANY] * len(after),
        out_specs=[VMEM] * pieces,
        out_shape=[shape] * pieces,
        compiler_params=pltpu.CompilerParams(vmem_limit_bytes=VMEM_LIMIT),
        cost_estimate=pl.CostEstimate(flops=size * len(parts), bytes_accessed=4 * size, transcendentals=0),
        name=name,
    )(*parts, *after)


def exchange(y_low, y_high, z_low, z_high):
    received = []
    for axis, low, high in (("gy", y_low, y_high), ("gz", z_low, z_high)):
        count = lax.axis_size(axis)
        up = [(i, i + 1) for i in range(count - 1)]
        down = [(i + 1, i) for i in range(count - 1)]
        received += [lax.ppermute(high, axis, up), lax.ppermute(low, axis, down)]
    return tuple(received)


def places(ring, pairs, share, order):
    rank = lax.axis_index("exp")
    row, half = rank // pairs, rank % pairs
    return [
        (((row + turn) % ring) * pairs + (half + swap) % pairs) * share + part * (share // 2)
        for turn, swap, part in order
    ]


def orders(ring):
    cross = [(turn, 1, 1) for turn in range(ring)]
    along = [(turn, swap, 0) for turn in (2, 1, 3) for swap in (1, 0)]
    own = [(0, 1, 0), (0, 0, 0)] + [(turn, 0, 1) for turn in range(ring)]
    return cross, along, own


def shards(ring, adjoint_final, concentration, observed, capacity, pore_mask, feed_index, feed_affinity):
    ranks = lax.axis_size("exp")
    pairs = ranks // ring
    adjoint = adjoint_final[0]
    nx, ny, nz = adjoint.shape
    share = nx // ranks
    planes = share // 2
    filled = concentration.reshape(-1, ny, nz)
    seen = observed.reshape(-1, ny, nz)

    def send(value, turn, swap):
        perm = [
            (r * pairs + h, ((r + turn) % ring) * pairs + (h + swap) % pairs) for r in range(ring) for h in range(pairs)
        ]
        return lax.ppermute(value, "exp", perm)

    scalars = (feed_index, feed_affinity)
    at = [functools.partial(places, ring, pairs, share, order) for order in orders(ring)]
    fields = (capacity, filled, seen)

    masked, wide, *outer = faces(adjoint, pore_mask)
    halo = exchange(*outer)
    state = (masked, weigh(wide))
    state, (cross,) = stage(scalars, fields, halo, state, at[0], (4,), planes, UNROLL, "cross")
    crossed = send(cross, 0, 1)
    state, along = stage(scalars, fields, halo, state, at[1], (2, 2, 2), planes, UNROLL, "along")
    parts_p = [send(value, turn, 0) for value, turn in zip(along, (2, 1, 3))]
    (_, kept, next_adjoint, *next_faces), (own_p, own_q) = stage(scalars, fields, halo, state, at[2], (2, 4), planes, UNROLL, "own")
    face_halo = exchange(*next_faces)

    totals_q = add([own_q, crossed], face_halo, ring, "add_q")
    parts_q = [send(totals_q[turn], turn, 0) for turn in (2, 1, 3)]
    total_s, total_k = add([own_p, *parts_p], totals_q[:1], 2, "add_p")
    last_p = send(total_s, 0, 1)
    adjoint_first = last_step(next_adjoint, kept, filled, seen, face_halo, total_k)

    sum_q = totals_q[0] + parts_q[0] + parts_q[1] + parts_q[2]
    return adjoint_first[None], jnp.concatenate([total_k + last_p, sum_q], 0)


def solution(mesh):
    in_specs = (
        P("exp", None, "gy", "gz"),
        P(None, "exp", None, "gy", "gz"),
        P(None, "exp", None, "gy", "gz"),
        P(None, "gy", "gz"),
        P(None, "gy", "gz"),
        P("exp"),
        P(),
    )
    out_specs = (P("exp", None, "gy", "gz"), P("exp", "gy", "gz"))
    return jax.shard_map(
        functools.partial(shards, 4), mesh=mesh, in_specs=in_specs, out_specs=out_specs, check_vma=False
    )
```

```python
import functools

import jax
import jax.numpy as jnp
from jax import lax
from jax.experimental import pallas as pl
from jax.experimental.pallas import tpu as pltpu
from jax.sharding import PartitionSpec as P

F32 = jnp.float32
SOLID = float("inf")
VMEM_LIMIT = 16 * 1024 * 1024
LANES = 128
ROWS = 8
UNROLL = (8, 4)
VMEM = pl.BlockSpec(memory_space=pltpu.VMEM)
ANY = pl.BlockSpec(memory_space=pl.ANY)
SMEM = pl.BlockSpec(memory_space=pltpu.SMEM)
HBM = pl.BlockSpec(memory_space=pltpu.HBM)


def lane_to(values, source, target):
    shift = target - source
    if isinstance(shift, int):
        return pltpu.roll(values, shift % LANES, 1)
    return pltpu.roll(values, lax.rem(shift + LANES, LANES), 1)


def in_hbm(*arrays):
    return [pltpu.with_memory_space_constraint(a, pltpu.HBM) for a in arrays]


def in_vmem(*arrays):
    return [pltpu.with_memory_space_constraint(a, pltpu.VMEM) for a in arrays]


def over(planes, unroll, body, carry=()):
    def some(k, carry):
        stores = []
        for u in range(unroll):
            carry, more = body(k * unroll + u, carry)
            stores += more
        for ref, index, value in stores:
            ref[index] = value
        return carry

    if unroll == planes:
        return some(0, carry)
    return lax.fori_loop(0, planes // unroll, some, carry)


def run(h):
    return slice(h * LANES, (h + 1) * LANES)


def padded_shape(nx, ny, nz):
    return (nz // LANES, nx + 2, ny + 2 * ROWS, LANES)


def halo_rows(wide, x, low, high):
    ny = wide.shape[2] - 2 * ROWS
    stores = []
    for h in range(wide.shape[0]):
        stores.append((wide, (h, x + 1, slice(ROWS - 1, ROWS)), low[:, run(h)]))
        stores.append((wide, (h, x + 1, slice(ROWS + ny, ROWS + ny + 1)), high[:, run(h)]))
    return stores


def face_rows(wide, x, row):
    count, planes, rows, _ = wide.shape
    flat = wide.reshape(count, planes * rows, LANES)
    return [flat[h, pl.ds((x + 1) * rows + ROWS + row, ROWS, stride=rows), :] for h in range(count)]


def store_rows(face, x, values, *lead):
    at = pl.ds(pl.multiple_of(x, ROWS), ROWS)
    for h, value in enumerate(values):
        face[(*lead, at, run(h))] = value


def weighted(wide, at, lane, z_low, z_high):
    count, _, rows, _ = wide.shape
    ny = rows - 2 * ROWS
    inner = slice(ROWS, ROWS + ny)
    centre = [wide[h, at, inner, :] for h in range(count)]
    ups = [pltpu.roll(c, 1, 1) for c in centre]
    downs = [pltpu.roll(c, LANES - 1, 1) for c in centre]
    sums = []
    for h in range(count):
        total = wide[h, at, ROWS - 1 : ROWS - 1 + ny, :] + wide[h, at, ROWS + 1 : ROWS + 1 + ny, :]
        total = total + (wide[h, at - 1, inner, :] + 3.0 * wide[h, at + 1, inner, :])
        left = jnp.where(lane == 0, ups[h - 1] if h else z_low, ups[h])
        right = jnp.where(lane == LANES - 1, downs[h + 1] if h + 1 < count else z_high, downs[h])
        sums.append(total + (left + right))
    return centre, sums


def rotating(steps, copies, body):
    for copy in copies(0, 0):
        copy.start()
    for t in range(steps):
        slot = t % 2
        if t + 1 < steps:
            for copy in copies(t + 1, 1 - slot):
                copy.start()
        for copy in copies(t, slot):
            copy.wait()
        body(t, slot)


def faces_kernel(planes, unroll, adj_hbm, pore_hbm, masked, wide, y_low, y_high, z_low, z_high, adj, pore, sem):
    nx, ny, nz = adj_hbm.shape
    count = nz // LANES
    lane = lax.broadcasted_iota(jnp.int32, (ny, LANES), 1)
    steps = nx // planes

    for h in range(count):
        for x in (0, nx + 1):
            masked[h, x] = jnp.zeros_like(masked[h, x])
            wide[h, x] = jnp.zeros_like(wide[h, x])

    def copies(t, slot):
        at = pl.ds(t * planes, planes)
        return [
            pltpu.make_async_copy(adj_hbm.at[at], adj.at[slot], sem.at[slot, 0]),
            pltpu.make_async_copy(pore_hbm.at[at], pore.at[slot], sem.at[slot, 1]),
        ]

    def body(t, slot):
        def load(i, carry):
            x = t * planes + i
            here = lane == x
            out = list(carry)
            stores = []
            for h in range(count):
                pores = pore[slot, i, :, run(h)].astype(F32)
                for part, (array, value) in enumerate(((masked, adj[slot, i, :, run(h)] * pores), (wide, pores))):
                    stores.append((array, (h, x + 1, slice(ROWS, ROWS + ny)), value))
                    if h == 0:
                        out[part] = jnp.where(here, lane_to(value, 0, x), out[part])
                    if h == count - 1:
                        out[2 + part] = jnp.where(here, lane_to(value, LANES - 1, x), out[2 + part])
                for rows in (slice(0, ROWS), slice(ROWS + ny, 2 * ROWS + ny)):
                    stores.append((wide, (h, x + 1, rows), jnp.zeros((ROWS, LANES), F32)))
            return tuple(out), stores

        parts = (z_low[:ny], z_low[ny:], z_high[:ny], z_high[ny:])
        z_low[:ny], z_low[ny:], z_high[:ny], z_high[ny:] = over(planes, unroll, load, parts)

        for x in range(t * planes, (t + 1) * planes, ROWS):
            for part, array in enumerate((masked, wide)):
                store_rows(y_low, x, face_rows(array, x, 0), part)
                store_rows(y_high, x, face_rows(array, x, ny - 1), part)

    rotating(steps, copies, body)


def faces(adjoint, pores, planes=16, unroll=16):
    nx, ny, nz = adjoint.shape
    y_shape = jax.ShapeDtypeStruct((2, nx, nz), F32)
    z_shape = jax.ShapeDtypeStruct((2 * ny, nx), F32)
    wide = padded_shape(nx, ny, nz)
    return pl.pallas_call(
        functools.partial(faces_kernel, planes, unroll),
        in_specs=[HBM, HBM],
        out_specs=[VMEM] * 6,
        out_shape=[pltpu.VMEM(wide, F32), pltpu.VMEM(wide, F32), y_shape, y_shape, z_shape, z_shape],
        scratch_shapes=[
            pltpu.VMEM((2, planes, ny, nz), F32),
            pltpu.VMEM((2, planes, ny, nz), jnp.int32),
            pltpu.SemaphoreType.DMA((2, 2)),
        ],
        compiler_params=pltpu.CompilerParams(vmem_limit_bytes=VMEM_LIMIT),
        cost_estimate=pl.CostEstimate(flops=4 * nx * ny * nz, bytes_accessed=8 * nx * ny * nz, transcendentals=0),
        name="faces",
    )(*in_hbm(adjoint, pores))


def weigh_kernel(unroll, wide, kept):
    count, nx, ny, _ = kept.shape
    lane = lax.broadcasted_iota(jnp.int32, (ny, LANES), 1)
    zero = jnp.zeros((ny, LANES), F32)

    def body(x, carry):
        pores, sums = weighted(wide, x + 1, lane, zero, zero)
        outer = jnp.where(x == nx - 1, 0.8, 1.0)
        return carry, [
            (kept, (h, x), jnp.where(pores[h] > 0.0, outer - 0.1 * sums[h], SOLID)) for h in range(count)
        ]

    over(nx, unroll, body)


def weigh(wide, unroll=32):
    count, nx, rows, lanes = wide.shape
    shape = (count, nx - 2, rows - 2 * ROWS, lanes)
    voxels = shape[0] * shape[1] * shape[2] * shape[3]
    return pl.pallas_call(
        functools.partial(weigh_kernel, unroll),
        in_specs=[VMEM],
        out_specs=VMEM,
        out_shape=pltpu.VMEM(shape, F32),
        compiler_params=pltpu.CompilerParams(vmem_limit_bytes=VMEM_LIMIT),
        cost_estimate=pl.CostEstimate(flops=12 * voxels, bytes_accessed=12 * voxels, transcendentals=0),
        name="weigh",
    )(*in_vmem(wide))


def stage_kernel(places, counts, planes, unroll, fresh, *refs):
    which, affinities, cap_hbm, filled_hbm, seen_hbm, y_low, y_high, z_low, z_high = refs[:9]
    refs = refs[9 + (2 if fresh else 7) :]
    (masked, kept, adj, out_y_low, out_y_high, out_z_low, out_z_high), refs = refs[:7], refs[7:]
    outs, (cap, late_f, early_f, late_o, inflow, sem) = refs[:-6], refs[-6:]
    count, nx, ny, _ = kept.shape
    lane = lax.broadcasted_iota(jnp.int32, (ny, LANES), 1)
    starts = places()
    inverse = 1.0 / jnp.full((1, LANES), affinities[which[0]], F32)

    if fresh:
        for h in range(count):
            for x in (0, nx + 1):
                adj[h, x] = jnp.zeros_like(adj[h, x])

    def copies(t, slot):
        start = starts[t]
        pairs = [
            (cap_hbm, start, cap),
            (filled_hbm, start + nx, late_f),
            (filled_hbm, start, early_f),
            (seen_hbm, start + nx, late_o),
        ]
        return [
            pltpu.make_async_copy(src.at[pl.ds(at, planes)], dst.at[slot], sem.at[slot, k])
            for k, (src, at, dst) in enumerate(pairs)
        ]

    targets = [(out, k) for out, n in zip(outs, counts) for k in range(n)]

    def body(t, slot):
        start = starts[t]
        grad, block = targets[t]
        m_low, p_low = z_low[:ny], 0.1 * z_low[ny:]
        m_high, p_high = z_high[:ny], 0.1 * z_high[ny:]

        def ends(i, carry):
            x = start + i
            row = pl.ds(x, 1)
            stores = halo_rows(masked, x, y_low[0, row, :], y_high[0, row, :])
            low, high = 0.1 * y_low[1, row, :], 0.1 * y_high[1, row, :]
            for h in range(count):
                for rows, value in ((slice(0, 1), low), (slice(ny - 1, ny), high)):
                    stores.append((kept, (h, x, rows), kept[h, x, rows, :] - value[:, run(h)]))
            return carry, stores

        over(planes, planes, ends)

        def gather(i, carry):
            x = start + i
            _, sums = weighted(masked, x + 1, lane, lane_to(m_low, x, 0), lane_to(m_high, x, LANES - 1))
            return carry, [(inflow, (h, i), 0.1 * sums[h]) for h in range(count)]

        over(planes, unroll[0], gather)

        def plane(i, carry):
            low, high = carry
            x = start + i
            stores = []
            for h in range(count):
                centre = masked[h, x + 1, ROWS : ROWS + ny, :]
                filled = late_f[slot, i, :, run(h)].astype(F32)
                early = early_f[slot, i, :, run(h)].astype(F32)
                source = filled - late_o[slot, i, :, run(h)].astype(F32)
                late_r = pl.reciprocal(-inverse - filled, approx=True)
                early_r = pl.reciprocal(-inverse - early, approx=True)
                weight = kept[h, x]
                if h == 0:
                    weight = weight - jnp.where(lane == 0, lane_to(p_low, x, 0), 0.0)
                if h == count - 1:
                    weight = weight - jnp.where(lane == LANES - 1, lane_to(p_high, x, LANES - 1), 0.0)
                pore = weight != SOLID
                uptake = cap[slot, i, :, run(h)] * inverse
                updated = centre * (weight - uptake * (late_r * late_r)) + (inflow[h, i] + source)
                updated = jnp.where(pore, updated, 0.0)
                stores.append((kept, (h, x), jnp.where(pore, weight - uptake * (early_r * early_r), SOLID)))
                term = (filled * late_r) * centre + (early * early_r) * updated
                stores.append((grad, (block * planes + i, slice(None), run(h)), term))
                stores.append((adj, (h, x + 1, slice(ROWS, ROWS + ny)), updated))
                if h == 0:
                    low = jnp.where(lane == x, lane_to(updated, 0, x), low)
                if h == count - 1:
                    high = jnp.where(lane == x, lane_to(updated, LANES - 1, x), high)
            return (low, high), stores

        out_z_low[...], out_z_high[...] = over(planes, unroll[1], plane, (out_z_low[...], out_z_high[...]))
        for at in range(0, planes, ROWS):
            store_rows(out_y_low, start + at, face_rows(adj, start + at, 0))
            store_rows(out_y_high, start + at, face_rows(adj, start + at, ny - 1))

    rotating(sum(counts), copies, body)


def stage(scalars, fields, halo, state, places, counts, planes, unroll, name):
    capacity, filled, seen = fields
    nx, ny, nz = capacity.shape
    runs = sum(counts)
    operands = [*scalars, *in_hbm(capacity, filled, seen), *halo, *in_vmem(*state)]
    base = len(operands) - len(state)
    shapes = [padded_shape(nx, ny, nz), (nz // LANES, nx, ny, LANES), padded_shape(nx, ny, nz), (nx, nz), (nx, nz), (ny, nx), (ny, nx)]
    shapes += [(n * planes, ny, nz) for n in counts]
    block = (2, planes, ny, nz)
    voxels = runs * planes * ny * nz
    results = pl.pallas_call(
        functools.partial(stage_kernel, places, counts, planes, unroll, len(state) == 2),
        in_specs=[SMEM] * 2 + [HBM] * 3 + [VMEM] * (4 + len(state)),
        out_specs=[VMEM] * len(shapes),
        out_shape=[pltpu.VMEM(s, F32) for s in shapes[:7]] + [jax.ShapeDtypeStruct(s, F32) for s in shapes[7:]],
        scratch_shapes=[
            pltpu.VMEM(block, F32),
            pltpu.VMEM(block, jnp.bfloat16),
            pltpu.VMEM(block, jnp.bfloat16),
            pltpu.VMEM(block, jnp.bfloat16),
            pltpu.VMEM((nz // LANES, planes, ny, LANES), F32),
            pltpu.SemaphoreType.DMA((2, 4)),
        ],
        input_output_aliases={base + k: k for k in range(len(state))},
        compiler_params=pltpu.CompilerParams(vmem_limit_bytes=VMEM_LIMIT),
        cost_estimate=pl.CostEstimate(flops=40 * voxels, bytes_accessed=10 * voxels, transcendentals=2 * voxels),
        name=name,
    )(*operands)
    return results[:7], results[7:]


def last_kernel(planes, unroll, f_hbm, o_hbm, kept, y_low, y_high, z_low, z_high, _, _after, out_hbm, adj, filled, seen, out, sem, out_sem):
    count, nx, ny, _ = kept.shape
    lane = lax.broadcasted_iota(jnp.int32, (ny, LANES), 1)
    steps = nx // planes

    def copies(t, slot):
        at = pl.ds(t * planes, planes)
        return [
            pltpu.make_async_copy(f_hbm.at[at], filled.at[slot], sem.at[slot, 0]),
            pltpu.make_async_copy(o_hbm.at[at], seen.at[slot], sem.at[slot, 1]),
        ]

    def writing(t):
        return pltpu.make_async_copy(out.at[t % 2], out_hbm.at[pl.ds(t * planes, planes)], out_sem.at[t % 2])

    def body(t, slot):
        if t >= 2:
            writing(t - 2).wait()

        def ends(i, carry):
            x = t * planes + i
            row = pl.ds(x, 1)
            return carry, halo_rows(adj, x, y_low[row, :], y_high[row, :])

        over(planes, planes, ends)

        def plane(i, carry):
            x = t * planes + i
            centre, sums = weighted(adj, x + 1, lane, lane_to(z_low[...], x, 0), lane_to(z_high[...], x, LANES - 1))
            stores = []
            for h in range(count):
                weight = kept[h, x]
                source = filled[slot, i, :, run(h)].astype(F32) - seen[slot, i, :, run(h)].astype(F32)
                value = centre[h] * weight + (0.1 * sums[h] + source)
                stores.append((out, (slot, i, slice(None), run(h)), jnp.where(weight == SOLID, 0.0, value)))
            return carry, stores

        over(planes, unroll, plane)
        writing(t).start()

    rotating(steps, copies, body)
    writing(steps - 2).wait()
    writing(steps - 1).wait()


def last_step(adjoint, kept, filled, seen, halo, after, planes=16, unroll=16):
    count, nx, ny, lanes = kept.shape
    nz = count * lanes
    voxels = nx * ny * nz
    return pl.pallas_call(
        functools.partial(last_kernel, planes, unroll),
        in_specs=[HBM, HBM] + [VMEM] * 6 + [ANY],
        out_specs=[HBM, VMEM],
        out_shape=[jax.ShapeDtypeStruct((nx, ny, nz), F32), pltpu.VMEM(adjoint.shape, F32)],
        scratch_shapes=[
            pltpu.VMEM((2, planes, ny, nz), jnp.bfloat16),
            pltpu.VMEM((2, planes, ny, nz), jnp.bfloat16),
            pltpu.VMEM((2, planes, ny, nz), F32),
            pltpu.SemaphoreType.DMA((2, 2)),
            pltpu.SemaphoreType.DMA((2,)),
        ],
        input_output_aliases={7: 1},
        compiler_params=pltpu.CompilerParams(vmem_limit_bytes=VMEM_LIMIT),
        cost_estimate=pl.CostEstimate(flops=20 * voxels, bytes_accessed=8 * voxels, transcendentals=0),
        name="last_step",
    )(*in_hbm(filled, seen), *in_vmem(kept), *halo, *in_vmem(adjoint), after)[0]


def add_kernel(n_parts, n_after, unroll, *refs):
    parts, outs = refs[:n_parts], refs[n_parts + n_after :]
    planes = outs[0].shape[0]

    def body(i, carry):
        stores = []
        for k, out in enumerate(outs):
            total = parts[0][k * planes + i]
            for part in parts[1:]:
                total = total + part[k * planes + i]
            stores.append((out, (i,), total))
        return carry, stores

    over(planes, unroll, body)


def add(parts, after, pieces, name, unroll=2):
    planes, ny, nz = parts[0].shape
    shape = jax.ShapeDtypeStruct((planes // pieces, ny, nz), F32)
    size = planes * ny * nz
    return pl.pallas_call(
        functools.partial(add_kernel, len(parts), len(after), unroll),
        in_specs=[VMEM] * len(parts) + [ANY] * len(after),
        out_specs=[VMEM] * pieces,
        out_shape=[shape] * pieces,
        compiler_params=pltpu.CompilerParams(vmem_limit_bytes=VMEM_LIMIT),
        cost_estimate=pl.CostEstimate(flops=size * len(parts), bytes_accessed=4 * size, transcendentals=0),
        name=name,
    )(*parts, *after)


def join_kernel(unroll, low, high, low_got, high_got, low_out, high_out):
    planes = low_got.shape[0]

    def body(i, carry):
        return carry, [
            (out, (((part + turned) % 2) * planes + i,), base[planes + i] if part else base[i] + got[i])
            for base, got, out, turned in ((low, low_got, low_out, 0), (high, high_got, high_out, 1))
            for part in (0, 1)
        ]

    over(planes, unroll, body)


def join(low, high, low_got, high_got, unroll=2):
    size = low.size
    return pl.pallas_call(
        functools.partial(join_kernel, unroll),
        in_specs=[VMEM] * 4,
        out_specs=[VMEM] * 2,
        out_shape=[jax.ShapeDtypeStruct(low.shape, F32)] * 2,
        compiler_params=pltpu.CompilerParams(vmem_limit_bytes=VMEM_LIMIT),
        cost_estimate=pl.CostEstimate(flops=size, bytes_accessed=4 * size, transcendentals=0),
        name="join",
    )(low, high, low_got, high_got)


def exchange(y_low, y_high, z_low, z_high):
    received = []
    for axis, low, high in (("gy", y_low, y_high), ("gz", z_low, z_high)):
        count = lax.axis_size(axis)
        up = [(i, i + 1) for i in range(count - 1)]
        down = [(i + 1, i) for i in range(count - 1)]
        received += [lax.ppermute(high, axis, up), lax.ppermute(low, axis, down)]
    return tuple(received)


def places(ring, pairs, share, order):
    rank = lax.axis_index("exp")
    row, half = rank // pairs, rank % pairs
    return [
        (((row + turn) % ring) * pairs + (half + swap) % pairs) * share + part * (share // 2)
        for turn, swap, part in order
    ]


def orders(ring):
    cross = [(turn, 1, 1) for turn in range(ring)]
    far = [(2, 1, 0), (2, 0, 0)]
    near = [(1, 1, 0), (1, 0, 0), (3, 0, 0), (3, 1, 0)]
    own = [(0, 1, 0), (0, 0, 0)] + [(turn, 0, 1) for turn in range(ring)]
    return cross, far, near, own


def shards(ring, adjoint_final, concentration, observed, capacity, pore_mask, feed_index, feed_affinity):
    ranks = lax.axis_size("exp")
    pairs = ranks // ring
    adjoint = adjoint_final[0]
    nx, ny, nz = adjoint.shape
    share = nx // ranks
    planes = share // 2
    filled = concentration.reshape(-1, ny, nz)
    seen = observed.reshape(-1, ny, nz)

    def send(value, turn, swap):
        perm = [
            (r * pairs + h, ((r + turn) % ring) * pairs + (h + swap) % pairs) for r in range(ring) for h in range(pairs)
        ]
        return lax.ppermute(value, "exp", perm)

    scalars = (feed_index, feed_affinity)
    at = [functools.partial(places, ring, pairs, share, order) for order in orders(ring)]
    fields = (capacity, filled, seen)

    masked, wide, *outer = faces(adjoint, pore_mask)
    halo = exchange(*outer)
    state = (masked, weigh(wide))
    state, (cross,) = stage(scalars, fields, halo, state, at[0], (4,), planes, UNROLL, "cross")
    crossed = send(cross, 0, 1)
    state, (far_s, far_k) = stage(scalars, fields, halo, state, at[1], (1, 1), planes, UNROLL, "far")
    got_s, got_k = send(far_s, 1, 0), send(far_k, 3, 0)
    state, (up, down) = stage(scalars, fields, halo, state, at[2], (2, 2), planes, UNROLL, "near")
    up, down = join(up, down, got_s, got_k)
    from_low, from_high = send(up, 1, 0), send(down, 3, 0)
    (_, kept, next_adjoint, *next_faces), (own_p, own_q) = stage(
        scalars, fields, halo, state, at[3], (2, 4), planes, UNROLL, "own"
    )
    face_halo = exchange(*next_faces)

    totals_q = add([own_q, crossed], face_halo, ring, "add_q")
    parts_q = [send(totals_q[turn], turn, 0) for turn in (2, 1, 3)]
    total_s, total_k = add([own_p, from_low, from_high], totals_q[:1], 2, "add_p")
    last_p = send(total_s, 0, 1)
    adjoint_first = last_step(next_adjoint, kept, filled, seen, face_halo, total_k)

    sum_q = totals_q[0] + parts_q[0] + parts_q[1] + parts_q[2]
    return adjoint_first[None], jnp.concatenate([total_k + last_p, sum_q], 0)


def solution(mesh):
    in_specs = (
        P("exp", None, "gy", "gz"),
        P(None, "exp", None, "gy", "gz"),
        P(None, "exp", None, "gy", "gz"),
        P(None, "gy", "gz"),
        P(None, "gy", "gz"),
        P("exp"),
        P(),
    )
    out_specs = (P("exp", None, "gy", "gz"), P("exp", "gy", "gz"))
    return jax.shard_map(
        functools.partial(shards, 4), mesh=mesh, in_specs=in_specs, out_specs=out_specs, check_vma=False
    )
```

```python
import functools

import jax
import jax.numpy as jnp
from jax import lax
from jax.experimental import pallas as pl
from jax.experimental.pallas import tpu as pltpu
from jax.sharding import PartitionSpec as P

F32 = jnp.float32
SOLID = float("inf")
VMEM_LIMIT = 16 * 1024 * 1024
LANES = 128
ROWS = 8
UNROLL = (8, 4)
VMEM = pl.BlockSpec(memory_space=pltpu.VMEM)
ANY = pl.BlockSpec(memory_space=pl.ANY)
SMEM = pl.BlockSpec(memory_space=pltpu.SMEM)
HBM = pl.BlockSpec(memory_space=pltpu.HBM)


def lane_to(values, source, target):
    shift = target - source
    if isinstance(shift, int):
        return pltpu.roll(values, shift % LANES, 1)
    return pltpu.roll(values, lax.rem(shift + LANES, LANES), 1)


def in_hbm(*arrays):
    return [pltpu.with_memory_space_constraint(a, pltpu.HBM) for a in arrays]


def in_vmem(*arrays):
    return [pltpu.with_memory_space_constraint(a, pltpu.VMEM) for a in arrays]


def over(planes, unroll, body, carry=()):
    def some(k, carry):
        stores = []
        for u in range(unroll):
            carry, more = body(k * unroll + u, carry)
            stores += more
        for ref, index, value in stores:
            ref[index] = value
        return carry

    if unroll == planes:
        return some(0, carry)
    return lax.fori_loop(0, planes // unroll, some, carry)


def run(h):
    return slice(h * LANES, (h + 1) * LANES)


def padded_shape(nx, ny, nz):
    return (nz // LANES, nx + 2, ny + 2 * ROWS, LANES)


def rows_of(array, x, row):
    rows = array.shape[2]
    return pl.ds(x * rows + row, ROWS, stride=rows)


def flat_rows(array):
    count, planes, rows, lanes = array.shape
    return array.reshape(count, planes * rows, lanes)


def halo_rows(wide, x, low, high):
    ny = wide.shape[2] - 2 * ROWS
    flat = flat_rows(wide)
    for h in range(wide.shape[0]):
        flat[h, rows_of(wide, x + 1, ROWS - 1), :] = low[:, run(h)]
        flat[h, rows_of(wide, x + 1, ROWS + ny), :] = high[:, run(h)]


def face_rows(wide, x, row):
    count, planes, rows, _ = wide.shape
    flat = wide.reshape(count, planes * rows, LANES)
    return [flat[h, pl.ds((x + 1) * rows + ROWS + row, ROWS, stride=rows), :] for h in range(count)]


def store_rows(face, x, values, *lead):
    at = pl.ds(pl.multiple_of(x, ROWS), ROWS)
    for h, value in enumerate(values):
        face[(*lead, at, run(h))] = value


def weighted(wide, at, lane, z_low, z_high):
    count, _, rows, _ = wide.shape
    ny = rows - 2 * ROWS
    inner = slice(ROWS, ROWS + ny)
    centre = [wide[h, at, inner, :] for h in range(count)]
    ups = [pltpu.roll(c, 1, 1) for c in centre]
    downs = [pltpu.roll(c, LANES - 1, 1) for c in centre]
    sums = []
    for h in range(count):
        total = wide[h, at, ROWS - 1 : ROWS - 1 + ny, :] + wide[h, at, ROWS + 1 : ROWS + 1 + ny, :]
        total = total + (wide[h, at - 1, inner, :] + 3.0 * wide[h, at + 1, inner, :])
        left = jnp.where(lane == 0, ups[h - 1] if h else z_low, ups[h])
        right = jnp.where(lane == LANES - 1, downs[h + 1] if h + 1 < count else z_high, downs[h])
        sums.append(total + (left + right))
    return centre, sums


def rotating(steps, copies, body, ahead=lambda t: None):
    for copy in copies(0, 0):
        copy.start()
    for t in range(steps):
        slot = t % 2
        if t + 1 < steps:
            for copy in copies(t + 1, 1 - slot):
                copy.start()
        ahead(t)
        for copy in copies(t, slot):
            copy.wait()
        body(t, slot)


def faces_kernel(planes, unroll, adj_hbm, pore_hbm, masked, wide, y_low, y_high, z_low, z_high, adj, pore, sem):
    nx, ny, nz = adj_hbm.shape
    count = nz // LANES
    lane = lax.broadcasted_iota(jnp.int32, (ny, LANES), 1)
    steps = nx // planes

    for h in range(count):
        for x in (0, nx + 1):
            masked[h, x] = jnp.zeros_like(masked[h, x])
            wide[h, x] = jnp.zeros_like(wide[h, x])

    def copies(t, slot):
        at = pl.ds(t * planes, planes)
        return [
            pltpu.make_async_copy(adj_hbm.at[at], adj.at[slot], sem.at[slot, 0]),
            pltpu.make_async_copy(pore_hbm.at[at], pore.at[slot], sem.at[slot, 1]),
        ]

    def body(t, slot):
        def load(i, carry):
            x = t * planes + i
            here = lane == x
            out = list(carry)
            stores = []
            for h in range(count):
                pores = pore[slot, i, :, run(h)].astype(F32)
                for part, (array, value) in enumerate(((masked, adj[slot, i, :, run(h)] * pores), (wide, pores))):
                    stores.append((array, (h, x + 1, slice(ROWS, ROWS + ny)), value))
                    if h == 0:
                        out[part] = jnp.where(here, lane_to(value, 0, x), out[part])
                    if h == count - 1:
                        out[2 + part] = jnp.where(here, lane_to(value, LANES - 1, x), out[2 + part])
                for rows in (slice(0, ROWS), slice(ROWS + ny, 2 * ROWS + ny)):
                    stores.append((wide, (h, x + 1, rows), jnp.zeros((ROWS, LANES), F32)))
            return tuple(out), stores

        parts = (z_low[:ny], z_low[ny:], z_high[:ny], z_high[ny:])
        z_low[:ny], z_low[ny:], z_high[:ny], z_high[ny:] = over(planes, unroll, load, parts)

        for x in range(t * planes, (t + 1) * planes, ROWS):
            for part, array in enumerate((masked, wide)):
                store_rows(y_low, x, face_rows(array, x, 0), part)
                store_rows(y_high, x, face_rows(array, x, ny - 1), part)

    rotating(steps, copies, body)


def faces(adjoint, pores, planes=16, unroll=16):
    nx, ny, nz = adjoint.shape
    y_shape = jax.ShapeDtypeStruct((2, nx, nz), F32)
    z_shape = jax.ShapeDtypeStruct((2 * ny, nx), F32)
    wide = padded_shape(nx, ny, nz)
    return pl.pallas_call(
        functools.partial(faces_kernel, planes, unroll),
        in_specs=[HBM, HBM],
        out_specs=[VMEM] * 6,
        out_shape=[pltpu.VMEM(wide, F32), pltpu.VMEM(wide, F32), y_shape, y_shape, z_shape, z_shape],
        scratch_shapes=[
            pltpu.VMEM((2, planes, ny, nz), F32),
            pltpu.VMEM((2, planes, ny, nz), jnp.int32),
            pltpu.SemaphoreType.DMA((2, 2)),
        ],
        compiler_params=pltpu.CompilerParams(vmem_limit_bytes=VMEM_LIMIT),
        cost_estimate=pl.CostEstimate(flops=4 * nx * ny * nz, bytes_accessed=8 * nx * ny * nz, transcendentals=0),
        name="faces",
    )(*in_hbm(adjoint, pores))


def weigh_kernel(unroll, wide, kept):
    count, nx, ny, _ = kept.shape
    lane = lax.broadcasted_iota(jnp.int32, (ny, LANES), 1)
    zero = jnp.zeros((ny, LANES), F32)

    def body(x, carry):
        pores, sums = weighted(wide, x + 1, lane, zero, zero)
        outer = jnp.where(x == nx - 1, 0.8, 1.0)
        return carry, [
            (kept, (h, x), jnp.where(pores[h] > 0.0, outer - 0.1 * sums[h], SOLID)) for h in range(count)
        ]

    over(nx, unroll, body)


def weigh(wide, unroll=32):
    count, nx, rows, lanes = wide.shape
    shape = (count, nx - 2, rows - 2 * ROWS, lanes)
    voxels = shape[0] * shape[1] * shape[2] * shape[3]
    return pl.pallas_call(
        functools.partial(weigh_kernel, unroll),
        in_specs=[VMEM],
        out_specs=VMEM,
        out_shape=pltpu.VMEM(shape, F32),
        compiler_params=pltpu.CompilerParams(vmem_limit_bytes=VMEM_LIMIT),
        cost_estimate=pl.CostEstimate(flops=12 * voxels, bytes_accessed=12 * voxels, transcendentals=0),
        name="weigh",
    )(*in_vmem(wide))


def stage_kernel(places, counts, planes, unroll, fresh, *refs):
    which, affinities, cap_hbm, filled_hbm, seen_hbm, y_low, y_high, z_low, z_high = refs[:9]
    refs = refs[9 + (2 if fresh else 7) :]
    (masked, kept, adj, out_y_low, out_y_high, out_z_low, out_z_high), refs = refs[:7], refs[7:]
    outs, (cap, late_f, early_f, late_o, inflow, sem) = refs[:-6], refs[-6:]
    count, nx, ny, _ = kept.shape
    lane = lax.broadcasted_iota(jnp.int32, (ny, LANES), 1)
    starts = places()
    inverse = 1.0 / jnp.full((1, LANES), affinities[which[0]], F32)

    if fresh:
        for h in range(count):
            for x in (0, nx + 1):
                adj[h, x] = jnp.zeros_like(adj[h, x])

    def copies(t, slot):
        start = starts[t]
        pairs = [
            (cap_hbm, start, cap),
            (filled_hbm, start + nx, late_f),
            (filled_hbm, start, early_f),
            (seen_hbm, start + nx, late_o),
        ]
        return [
            pltpu.make_async_copy(src.at[pl.ds(at, planes)], dst.at[slot], sem.at[slot, k])
            for k, (src, at, dst) in enumerate(pairs)
        ]

    targets = [(out, k) for out, n in zip(outs, counts) for k in range(n)]

    def ahead(t):
        start = starts[t]
        m_low, m_high = z_low[:ny], z_high[:ny]

        flat = flat_rows(kept)
        for at in range(0, planes, ROWS):
            x = pl.multiple_of(start + at, ROWS)
            halo_rows(masked, x, y_low[0, pl.ds(x, ROWS), :], y_high[0, pl.ds(x, ROWS), :])
            for row, side in ((0, y_low), (ny - 1, y_high)):
                taken = 0.1 * side[1, pl.ds(x, ROWS), :]
                for h in range(count):
                    index = rows_of(kept, x, row)
                    flat[h, index, :] = flat[h, index, :] - taken[:, run(h)]

        def gather(i, carry):
            x = start + i
            _, sums = weighted(masked, x + 1, lane, lane_to(m_low, x, 0), lane_to(m_high, x, LANES - 1))
            return carry, [(inflow, (h, i), 0.1 * sums[h]) for h in range(count)]

        over(planes, unroll[0], gather)

    def body(t, slot):
        start = starts[t]
        grad, block = targets[t]
        p_low, p_high = 0.1 * z_low[ny:], 0.1 * z_high[ny:]

        def plane(i, carry):
            low, high = carry
            x = start + i
            stores = []
            for h in range(count):
                centre = masked[h, x + 1, ROWS : ROWS + ny, :]
                filled = late_f[slot, i, :, run(h)].astype(F32)
                early = early_f[slot, i, :, run(h)].astype(F32)
                source = filled - late_o[slot, i, :, run(h)].astype(F32)
                late_r = pl.reciprocal(-inverse - filled, approx=True)
                early_r = pl.reciprocal(-inverse - early, approx=True)
                weight = kept[h, x]
                if h == 0:
                    weight = weight - jnp.where(lane == 0, lane_to(p_low, x, 0), 0.0)
                if h == count - 1:
                    weight = weight - jnp.where(lane == LANES - 1, lane_to(p_high, x, LANES - 1), 0.0)
                pore = weight != SOLID
                uptake = cap[slot, i, :, run(h)] * inverse
                updated = centre * (weight - uptake * (late_r * late_r)) + (inflow[h, i] + source)
                updated = jnp.where(pore, updated, 0.0)
                stores.append((kept, (h, x), jnp.where(pore, weight - uptake * (early_r * early_r), SOLID)))
                term = (filled * late_r) * centre + (early * early_r) * updated
                stores.append((grad, (block * planes + i, slice(None), run(h)), term))
                stores.append((adj, (h, x + 1, slice(ROWS, ROWS + ny)), updated))
                if h == 0:
                    low = jnp.where(lane == x, lane_to(updated, 0, x), low)
                if h == count - 1:
                    high = jnp.where(lane == x, lane_to(updated, LANES - 1, x), high)
            return (low, high), stores

        out_z_low[...], out_z_high[...] = over(planes, unroll[1], plane, (out_z_low[...], out_z_high[...]))
        for at in range(0, planes, ROWS):
            store_rows(out_y_low, start + at, face_rows(adj, start + at, 0))
            store_rows(out_y_high, start + at, face_rows(adj, start + at, ny - 1))

    rotating(sum(counts), copies, body, ahead)


def stage(scalars, fields, halo, state, places, counts, planes, unroll, name):
    capacity, filled, seen = fields
    nx, ny, nz = capacity.shape
    runs = sum(counts)
    operands = [*scalars, *in_hbm(capacity, filled, seen), *halo, *in_vmem(*state)]
    base = len(operands) - len(state)
    shapes = [padded_shape(nx, ny, nz), (nz // LANES, nx, ny, LANES), padded_shape(nx, ny, nz), (nx, nz), (nx, nz), (ny, nx), (ny, nx)]
    shapes += [(n * planes, ny, nz) for n in counts]
    block = (2, planes, ny, nz)
    voxels = runs * planes * ny * nz
    results = pl.pallas_call(
        functools.partial(stage_kernel, places, counts, planes, unroll, len(state) == 2),
        in_specs=[SMEM] * 2 + [HBM] * 3 + [VMEM] * (4 + len(state)),
        out_specs=[VMEM] * len(shapes),
        out_shape=[pltpu.VMEM(s, F32) for s in shapes[:7]] + [jax.ShapeDtypeStruct(s, F32) for s in shapes[7:]],
        scratch_shapes=[
            pltpu.VMEM(block, F32),
            pltpu.VMEM(block, jnp.bfloat16),
            pltpu.VMEM(block, jnp.bfloat16),
            pltpu.VMEM(block, jnp.bfloat16),
            pltpu.VMEM((nz // LANES, planes, ny, LANES), F32),
            pltpu.SemaphoreType.DMA((2, 4)),
        ],
        input_output_aliases={base + k: k for k in range(len(state))},
        compiler_params=pltpu.CompilerParams(vmem_limit_bytes=VMEM_LIMIT),
        cost_estimate=pl.CostEstimate(flops=40 * voxels, bytes_accessed=10 * voxels, transcendentals=2 * voxels),
        name=name,
    )(*operands)
    return results[:7], results[7:]


def last_kernel(planes, unroll, f_hbm, o_hbm, kept, y_low, y_high, z_low, z_high, _, _after, out_hbm, adj, filled, seen, out, inflow, sem, out_sem):
    count, nx, ny, _ = kept.shape
    lane = lax.broadcasted_iota(jnp.int32, (ny, LANES), 1)
    steps = nx // planes

    def copies(t, slot):
        at = pl.ds(t * planes, planes)
        return [
            pltpu.make_async_copy(f_hbm.at[at], filled.at[slot], sem.at[slot, 0]),
            pltpu.make_async_copy(o_hbm.at[at], seen.at[slot], sem.at[slot, 1]),
        ]

    def writing(t):
        return pltpu.make_async_copy(out.at[t % 2], out_hbm.at[pl.ds(t * planes, planes)], out_sem.at[t % 2])

    def ahead(t):
        for x in range(t * planes, (t + 1) * planes, ROWS):
            halo_rows(adj, x, y_low[pl.ds(x, ROWS), :], y_high[pl.ds(x, ROWS), :])

        def gather(i, carry):
            x = t * planes + i
            low, high = lane_to(z_low[...], x, 0), lane_to(z_high[...], x, LANES - 1)
            _, sums = weighted(adj, x + 1, lane, low, high)
            return carry, [(inflow, (h, i), 0.1 * sums[h]) for h in range(count)]

        over(planes, planes, gather)

    def body(t, slot):
        if t >= 2:
            writing(t - 2).wait()

        def plane(i, carry):
            x = t * planes + i
            stores = []
            for h in range(count):
                weight = kept[h, x]
                centre = adj[h, x + 1, ROWS : ROWS + ny, :]
                source = filled[slot, i, :, run(h)].astype(F32) - seen[slot, i, :, run(h)].astype(F32)
                value = centre * weight + (inflow[h, i] + source)
                stores.append((out, (slot, i, slice(None), run(h)), jnp.where(weight == SOLID, 0.0, value)))
            return carry, stores

        over(planes, unroll, plane)
        writing(t).start()

    rotating(steps, copies, body, ahead)
    writing(steps - 2).wait()
    writing(steps - 1).wait()


def last_step(adjoint, kept, filled, seen, halo, after, planes=16, unroll=8):
    count, nx, ny, lanes = kept.shape
    nz = count * lanes
    voxels = nx * ny * nz
    return pl.pallas_call(
        functools.partial(last_kernel, planes, unroll),
        in_specs=[HBM, HBM] + [VMEM] * 6 + [ANY],
        out_specs=[HBM, VMEM],
        out_shape=[jax.ShapeDtypeStruct((nx, ny, nz), F32), pltpu.VMEM(adjoint.shape, F32)],
        scratch_shapes=[
            pltpu.VMEM((2, planes, ny, nz), jnp.bfloat16),
            pltpu.VMEM((2, planes, ny, nz), jnp.bfloat16),
            pltpu.VMEM((2, planes, ny, nz), F32),
            pltpu.VMEM((count, planes, ny, lanes), F32),
            pltpu.SemaphoreType.DMA((2, 2)),
            pltpu.SemaphoreType.DMA((2,)),
        ],
        input_output_aliases={7: 1},
        compiler_params=pltpu.CompilerParams(vmem_limit_bytes=VMEM_LIMIT),
        cost_estimate=pl.CostEstimate(flops=20 * voxels, bytes_accessed=8 * voxels, transcendentals=0),
        name="last_step",
    )(*in_hbm(filled, seen), *in_vmem(kept), *halo, *in_vmem(adjoint), after)[0]


def add_kernel(n_parts, n_after, unroll, *refs):
    parts, outs = refs[:n_parts], refs[n_parts + n_after :]
    planes = outs[0].shape[0]

    def body(i, carry):
        stores = []
        for k, out in enumerate(outs):
            total = parts[0][k * planes + i]
            for part in parts[1:]:
                total = total + part[k * planes + i]
            stores.append((out, (i,), total))
        return carry, stores

    over(planes, unroll, body)


def add(parts, after, pieces, name, unroll=2):
    planes, ny, nz = parts[0].shape
    shape = jax.ShapeDtypeStruct((planes // pieces, ny, nz), F32)
    size = planes * ny * nz
    return pl.pallas_call(
        functools.partial(add_kernel, len(parts), len(after), unroll),
        in_specs=[VMEM] * len(parts) + [ANY] * len(after),
        out_specs=[VMEM] * pieces,
        out_shape=[shape] * pieces,
        compiler_params=pltpu.CompilerParams(vmem_limit_bytes=VMEM_LIMIT),
        cost_estimate=pl.CostEstimate(flops=size * len(parts), bytes_accessed=4 * size, transcendentals=0),
        name=name,
    )(*parts, *after)


def join_kernel(unroll, low, high, low_got, high_got, low_out, high_out):
    planes = low_got.shape[0]

    def body(i, carry):
        return carry, [
            (out, (((part + turned) % 2) * planes + i,), base[planes + i] if part else base[i] + got[i])
            for base, got, out, turned in ((low, low_got, low_out, 0), (high, high_got, high_out, 1))
            for part in (0, 1)
        ]

    over(planes, unroll, body)


def join(low, high, low_got, high_got, unroll=2):
    size = low.size
    return pl.pallas_call(
        functools.partial(join_kernel, unroll),
        in_specs=[VMEM] * 4,
        out_specs=[VMEM] * 2,
        out_shape=[jax.ShapeDtypeStruct(low.shape, F32)] * 2,
        compiler_params=pltpu.CompilerParams(vmem_limit_bytes=VMEM_LIMIT),
        cost_estimate=pl.CostEstimate(flops=size, bytes_accessed=4 * size, transcendentals=0),
        name="join",
    )(low, high, low_got, high_got)


def exchange(y_low, y_high, z_low, z_high):
    received = []
    for axis, low, high in (("gy", y_low, y_high), ("gz", z_low, z_high)):
        count = lax.axis_size(axis)
        up = [(i, i + 1) for i in range(count - 1)]
        down = [(i + 1, i) for i in range(count - 1)]
        received += [lax.ppermute(high, axis, up), lax.ppermute(low, axis, down)]
    return tuple(received)


def places(ring, pairs, share, order):
    rank = lax.axis_index("exp")
    row, half = rank // pairs, rank % pairs
    return [
        (((row + turn) % ring) * pairs + (half + swap) % pairs) * share + part * (share // 2)
        for turn, swap, part in order
    ]


def orders(ring):
    cross = [(turn, 1, 1) for turn in range(ring)]
    far = [(2, 1, 0), (2, 0, 0)]
    near = [(1, 1, 0), (1, 0, 0), (3, 0, 0), (3, 1, 0)]
    own = [(0, 1, 0), (0, 0, 0)] + [(turn, 0, 1) for turn in range(ring)]
    return cross + far, near + own


def shards(ring, adjoint_final, concentration, observed, capacity, pore_mask, feed_index, feed_affinity):
    ranks = lax.axis_size("exp")
    pairs = ranks // ring
    adjoint = adjoint_final[0]
    nx, ny, nz = adjoint.shape
    share = nx // ranks
    planes = share // 2
    filled = concentration.reshape(-1, ny, nz)
    seen = observed.reshape(-1, ny, nz)

    def send(value, turn, swap):
        perm = [
            (r * pairs + h, ((r + turn) % ring) * pairs + (h + swap) % pairs) for r in range(ring) for h in range(pairs)
        ]
        return lax.ppermute(value, "exp", perm)

    scalars = (feed_index, feed_affinity)
    at = [functools.partial(places, ring, pairs, share, order) for order in orders(ring)]
    fields = (capacity, filled, seen)

    masked, wide, *outer = faces(adjoint, pore_mask)
    halo = exchange(*outer)
    state = (masked, weigh(wide))
    state, (cross, far_s, far_k) = stage(scalars, fields, halo, state, at[0], (4, 1, 1), planes, UNROLL, "early")
    crossed = send(cross, 0, 1)
    got_s, got_k = send(far_s, 1, 0), send(far_k, 3, 0)
    (_, kept, next_adjoint, *next_faces), (up, down, own_p, own_q) = stage(
        scalars, fields, halo, state, at[1], (2, 2, 2, 4), planes, UNROLL, "late"
    )
    up, down = join(up, down, got_s, got_k)
    from_low, from_high = send(up, 1, 0), send(down, 3, 0)
    face_halo = exchange(*next_faces)

    totals_q = add([own_q, crossed], face_halo, ring, "add_q")
    parts_q = [send(totals_q[turn], turn, 0) for turn in (2, 1, 3)]
    total_s, total_k = add([own_p, from_low, from_high], totals_q[:1], 2, "add_p")
    last_p = send(total_s, 0, 1)
    adjoint_first = last_step(next_adjoint, kept, filled, seen, face_halo, total_k)

    sum_q = totals_q[0] + parts_q[0] + parts_q[1] + parts_q[2]
    return adjoint_first[None], jnp.concatenate([total_k + last_p, sum_q], 0)


def solution(mesh):
    in_specs = (
        P("exp", None, "gy", "gz"),
        P(None, "exp", None, "gy", "gz"),
        P(None, "exp", None, "gy", "gz"),
        P(None, "gy", "gz"),
        P(None, "gy", "gz"),
        P("exp"),
        P(),
    )
    out_specs = (P("exp", None, "gy", "gz"), P("exp", "gy", "gz"))
    return jax.shard_map(
        functools.partial(shards, 4), mesh=mesh, in_specs=in_specs, out_specs=out_specs, check_vma=False
    )
```

```python
import functools

import jax
import jax.numpy as jnp
from jax import lax
from jax.experimental import pallas as pl
from jax.experimental.pallas import tpu as pltpu
from jax.sharding import PartitionSpec as P

F32 = jnp.float32
SOLID = float("inf")
VMEM_LIMIT = 16 * 1024 * 1024
LANES = 128
ROWS = 8
UNROLL = (8, 4)
VMEM = pl.BlockSpec(memory_space=pltpu.VMEM)
ANY = pl.BlockSpec(memory_space=pl.ANY)
SMEM = pl.BlockSpec(memory_space=pltpu.SMEM)
HBM = pl.BlockSpec(memory_space=pltpu.HBM)


def lane_to(values, source, target):
    shift = target - source
    if isinstance(shift, int):
        return pltpu.roll(values, shift % LANES, 1)
    return pltpu.roll(values, lax.rem(shift + LANES, LANES), 1)


def columns(low, high, x, lane):
    return lane_to(jnp.where(lane == x, low, high), x, 0)


def collect(values, x, lane, low, high):
    before = (x - 1) % LANES if isinstance(x, int) else lax.rem(x + LANES - 1, LANES)
    ends = lane_to(jnp.where(lane == 0, values[0], values[-1]), 0, x)
    return jnp.where(lane == x, ends, low), jnp.where(lane == before, ends, high)


def one_back(values):
    return pltpu.roll(values, LANES - 1, 1)


def one_on(values):
    return pltpu.roll(values, 1, 1)


def in_hbm(*arrays):
    return [pltpu.with_memory_space_constraint(a, pltpu.HBM) for a in arrays]


def in_vmem(*arrays):
    return [pltpu.with_memory_space_constraint(a, pltpu.VMEM) for a in arrays]


def over(planes, unroll, body, carry=()):
    def some(k, carry):
        stores = []
        for u in range(unroll):
            carry, more = body(k * unroll + u, carry)
            stores += more
        for ref, index, value in stores:
            ref[index] = value
        return carry

    if unroll == planes:
        return some(0, carry)
    return lax.fori_loop(0, planes // unroll, some, carry)


def run(h):
    return slice(h * LANES, (h + 1) * LANES)


def padded_shape(nx, ny, nz):
    return (nz // LANES, nx + 2, ny + 2 * ROWS, LANES)


def rows_of(array, x, row):
    rows = array.shape[2]
    return pl.ds(x * rows + row, ROWS, stride=rows)


def flat_rows(array):
    count, planes, rows, lanes = array.shape
    return array.reshape(count, planes * rows, lanes)


def halo_rows(wide, x, low, high):
    ny = wide.shape[2] - 2 * ROWS
    flat = flat_rows(wide)
    for h in range(wide.shape[0]):
        flat[h, rows_of(wide, x + 1, ROWS - 1), :] = low[:, run(h)]
        flat[h, rows_of(wide, x + 1, ROWS + ny), :] = high[:, run(h)]


def face_rows(wide, x, row):
    count, planes, rows, _ = wide.shape
    flat = wide.reshape(count, planes * rows, LANES)
    return [flat[h, pl.ds((x + 1) * rows + ROWS + row, ROWS, stride=rows), :] for h in range(count)]


def store_rows(face, x, values, *lead):
    at = pl.ds(pl.multiple_of(x, ROWS), ROWS)
    for h, value in enumerate(values):
        face[(*lead, at, run(h))] = value


def weighted(wide, at, lane, z_low, z_high):
    count, _, rows, _ = wide.shape
    ny = rows - 2 * ROWS
    inner = slice(ROWS, ROWS + ny)
    centre = [wide[h, at, inner, :] for h in range(count)]
    ups = [pltpu.roll(c, 1, 1) for c in centre]
    downs = [pltpu.roll(c, LANES - 1, 1) for c in centre]
    sums = []
    for h in range(count):
        total = wide[h, at, ROWS - 1 : ROWS - 1 + ny, :] + wide[h, at, ROWS + 1 : ROWS + 1 + ny, :]
        total = total + (wide[h, at - 1, inner, :] + 3.0 * wide[h, at + 1, inner, :])
        left = jnp.where(lane == 0, ups[h - 1] if h else z_low, ups[h])
        right = jnp.where(lane == LANES - 1, downs[h + 1] if h + 1 < count else z_high, downs[h])
        sums.append(total + (left + right))
    return centre, sums


def rotating(steps, copies, body, ahead=lambda t: None):
    for copy in copies(0, 0):
        copy.start()
    for t in range(steps):
        slot = t % 2
        if t + 1 < steps:
            for copy in copies(t + 1, 1 - slot):
                copy.start()
        ahead(t)
        for copy in copies(t, slot):
            copy.wait()
        body(t, slot)


def faces_kernel(planes, unroll, adj_hbm, pore_hbm, masked, wide, y_low, y_high, z_low, z_high, adj, pore, sem):
    nx, ny, nz = adj_hbm.shape
    count = nz // LANES
    lane = lax.broadcasted_iota(jnp.int32, (ny, LANES), 1)
    steps = nx // planes

    for h in range(count):
        for x in (0, nx + 1):
            masked[h, x] = jnp.zeros_like(masked[h, x])
            wide[h, x] = jnp.zeros_like(wide[h, x])

    def copies(t, slot):
        at = pl.ds(t * planes, planes)
        return [
            pltpu.make_async_copy(adj_hbm.at[at], adj.at[slot], sem.at[slot, 0]),
            pltpu.make_async_copy(pore_hbm.at[at], pore.at[slot], sem.at[slot, 1]),
        ]

    def body(t, slot):
        def load(i, carry):
            x = t * planes + i
            out = list(carry)
            stores, values = [], ([], [])
            for h in range(count):
                pores = pore[slot, i, :, run(h)].astype(F32)
                for part, (array, value) in enumerate(((masked, adj[slot, i, :, run(h)] * pores), (wide, pores))):
                    stores.append((array, (h, x + 1, slice(ROWS, ROWS + ny)), value))
                    values[part].append(value)
                for rows in (slice(0, ROWS), slice(ROWS + ny, 2 * ROWS + ny)):
                    stores.append((wide, (h, x + 1, rows), jnp.zeros((ROWS, LANES), F32)))
            for part in range(2):
                out[part], out[2 + part] = collect(values[part], x, lane, out[part], out[2 + part])
            return tuple(out), stores

        parts = (z_low[:ny], z_low[ny:], one_back(z_high[:ny]), one_back(z_high[ny:]))
        z_low[:ny], z_low[ny:], m_high, p_high = over(planes, unroll, load, parts)
        z_high[:ny], z_high[ny:] = one_on(m_high), one_on(p_high)

        for x in range(t * planes, (t + 1) * planes, ROWS):
            for part, array in enumerate((masked, wide)):
                store_rows(y_low, x, face_rows(array, x, 0), part)
                store_rows(y_high, x, face_rows(array, x, ny - 1), part)

    rotating(steps, copies, body)


def faces(adjoint, pores, planes=16, unroll=16):
    nx, ny, nz = adjoint.shape
    y_shape = jax.ShapeDtypeStruct((2, nx, nz), F32)
    z_shape = jax.ShapeDtypeStruct((2 * ny, nx), F32)
    wide = padded_shape(nx, ny, nz)
    return pl.pallas_call(
        functools.partial(faces_kernel, planes, unroll),
        in_specs=[HBM, HBM],
        out_specs=[VMEM] * 6,
        out_shape=[pltpu.VMEM(wide, F32), pltpu.VMEM(wide, F32), y_shape, y_shape, z_shape, z_shape],
        scratch_shapes=[
            pltpu.VMEM((2, planes, ny, nz), F32),
            pltpu.VMEM((2, planes, ny, nz), jnp.int32),
            pltpu.SemaphoreType.DMA((2, 2)),
        ],
        compiler_params=pltpu.CompilerParams(vmem_limit_bytes=VMEM_LIMIT),
        cost_estimate=pl.CostEstimate(flops=4 * nx * ny * nz, bytes_accessed=8 * nx * ny * nz, transcendentals=0),
        name="faces",
    )(*in_hbm(adjoint, pores))


def weigh_kernel(unroll, wide, kept):
    count, nx, ny, _ = kept.shape
    lane = lax.broadcasted_iota(jnp.int32, (ny, LANES), 1)
    zero = jnp.zeros((ny, LANES), F32)

    def body(x, carry):
        pores, sums = weighted(wide, x + 1, lane, zero, zero)
        outer = jnp.where(x == nx - 1, 0.8, 1.0)
        return carry, [
            (kept, (h, x), jnp.where(pores[h] > 0.0, outer - 0.1 * sums[h], SOLID)) for h in range(count)
        ]

    over(nx, unroll, body)


def weigh(wide, unroll=32):
    count, nx, rows, lanes = wide.shape
    shape = (count, nx - 2, rows - 2 * ROWS, lanes)
    voxels = shape[0] * shape[1] * shape[2] * shape[3]
    return pl.pallas_call(
        functools.partial(weigh_kernel, unroll),
        in_specs=[VMEM],
        out_specs=VMEM,
        out_shape=pltpu.VMEM(shape, F32),
        compiler_params=pltpu.CompilerParams(vmem_limit_bytes=VMEM_LIMIT),
        cost_estimate=pl.CostEstimate(flops=12 * voxels, bytes_accessed=12 * voxels, transcendentals=0),
        name="weigh",
    )(*in_vmem(wide))


def stage_kernel(places, counts, planes, unroll, fresh, *refs):
    which, affinities, cap_hbm, filled_hbm, seen_hbm, y_low, y_high, z_low, z_high = refs[:9]
    refs = refs[9 + (2 if fresh else 7) :]
    (masked, kept, adj, out_y_low, out_y_high, out_z_low, out_z_high), refs = refs[:7], refs[7:]
    outs, (cap, late_f, early_f, late_o, inflow, sem) = refs[:-6], refs[-6:]
    count, nx, ny, _ = kept.shape
    lane = lax.broadcasted_iota(jnp.int32, (ny, LANES), 1)
    starts = places()
    inverse = 1.0 / jnp.full((1, LANES), affinities[which[0]], F32)

    if fresh:
        for h in range(count):
            for x in (0, nx + 1):
                adj[h, x] = jnp.zeros_like(adj[h, x])

    def copies(t, slot):
        start = starts[t]
        pairs = [
            (cap_hbm, start, cap),
            (filled_hbm, start + nx, late_f),
            (filled_hbm, start, early_f),
            (seen_hbm, start + nx, late_o),
        ]
        return [
            pltpu.make_async_copy(src.at[pl.ds(at, planes)], dst.at[slot], sem.at[slot, k])
            for k, (src, at, dst) in enumerate(pairs)
        ]

    targets = [(out, k) for out, n in zip(outs, counts) for k in range(n)]

    def ahead(t):
        start = starts[t]
        m_low, m_high = z_low[:ny], one_back(z_high[:ny])

        flat = flat_rows(kept)
        for at in range(0, planes, ROWS):
            x = pl.multiple_of(start + at, ROWS)
            halo_rows(masked, x, y_low[0, pl.ds(x, ROWS), :], y_high[0, pl.ds(x, ROWS), :])
            for row, side in ((0, y_low), (ny - 1, y_high)):
                taken = 0.1 * side[1, pl.ds(x, ROWS), :]
                for h in range(count):
                    index = rows_of(kept, x, row)
                    flat[h, index, :] = flat[h, index, :] - taken[:, run(h)]

        def gather(i, carry):
            x = start + i
            beside = columns(m_low, m_high, x, lane)
            _, sums = weighted(masked, x + 1, lane, beside, beside)
            return carry, [(inflow, (h, i), 0.1 * sums[h]) for h in range(count)]

        over(planes, unroll[0], gather)

    def body(t, slot):
        start = starts[t]
        grad, block = targets[t]
        p_low, p_high = 0.1 * z_low[ny:], one_back(0.1 * z_high[ny:])

        def plane(i, carry):
            low, high = carry
            x = start + i
            beside = columns(p_low, p_high, x, lane)
            stores, values = [], []
            for h in range(count):
                centre = masked[h, x + 1, ROWS : ROWS + ny, :]
                filled = late_f[slot, i, :, run(h)].astype(F32)
                early = early_f[slot, i, :, run(h)].astype(F32)
                source = filled - late_o[slot, i, :, run(h)].astype(F32)
                late_r = pl.reciprocal(-inverse - filled, approx=True)
                early_r = pl.reciprocal(-inverse - early, approx=True)
                weight = kept[h, x]
                if h == 0:
                    weight = weight - jnp.where(lane == 0, beside, 0.0)
                if h == count - 1:
                    weight = weight - jnp.where(lane == LANES - 1, beside, 0.0)
                pore = weight != SOLID
                uptake = cap[slot, i, :, run(h)] * inverse
                updated = centre * (weight - uptake * (late_r * late_r)) + (inflow[h, i] + source)
                updated = jnp.where(pore, updated, 0.0)
                stores.append((kept, (h, x), jnp.where(pore, weight - uptake * (early_r * early_r), SOLID)))
                term = (filled * late_r) * centre + (early * early_r) * updated
                stores.append((grad, (block * planes + i, slice(None), run(h)), term))
                stores.append((adj, (h, x + 1, slice(ROWS, ROWS + ny)), updated))
                values.append(updated)
            return collect(values, x, lane, low, high), stores

        out_z_low[...], high = over(planes, unroll[1], plane, (out_z_low[...], one_back(out_z_high[...])))
        out_z_high[...] = one_on(high)
        for at in range(0, planes, ROWS):
            store_rows(out_y_low, start + at, face_rows(adj, start + at, 0))
            store_rows(out_y_high, start + at, face_rows(adj, start + at, ny - 1))

    rotating(sum(counts), copies, body, ahead)


def stage(scalars, fields, halo, state, places, counts, planes, unroll, name):
    capacity, filled, seen = fields
    nx, ny, nz = capacity.shape
    runs = sum(counts)
    operands = [*scalars, *in_hbm(capacity, filled, seen), *halo, *in_vmem(*state)]
    base = len(operands) - len(state)
    shapes = [padded_shape(nx, ny, nz), (nz // LANES, nx, ny, LANES), padded_shape(nx, ny, nz), (nx, nz), (nx, nz), (ny, nx), (ny, nx)]
    shapes += [(n * planes, ny, nz) for n in counts]
    block = (2, planes, ny, nz)
    voxels = runs * planes * ny * nz
    results = pl.pallas_call(
        functools.partial(stage_kernel, places, counts, planes, unroll, len(state) == 2),
        in_specs=[SMEM] * 2 + [HBM] * 3 + [VMEM] * (4 + len(state)),
        out_specs=[VMEM] * len(shapes),
        out_shape=[pltpu.VMEM(s, F32) for s in shapes[:7]] + [jax.ShapeDtypeStruct(s, F32) for s in shapes[7:]],
        scratch_shapes=[
            pltpu.VMEM(block, F32),
            pltpu.VMEM(block, jnp.bfloat16),
            pltpu.VMEM(block, jnp.bfloat16),
            pltpu.VMEM(block, jnp.bfloat16),
            pltpu.VMEM((nz // LANES, planes, ny, LANES), F32),
            pltpu.SemaphoreType.DMA((2, 4)),
        ],
        input_output_aliases={base + k: k for k in range(len(state))},
        compiler_params=pltpu.CompilerParams(vmem_limit_bytes=VMEM_LIMIT),
        cost_estimate=pl.CostEstimate(flops=40 * voxels, bytes_accessed=10 * voxels, transcendentals=2 * voxels),
        name=name,
    )(*operands)
    return results[:7], results[7:]


def last_kernel(planes, unroll, f_hbm, o_hbm, kept, y_low, y_high, z_low, z_high, _, _after, out_hbm, adj, filled, seen, out, inflow, sem, out_sem):
    count, nx, ny, _ = kept.shape
    lane = lax.broadcasted_iota(jnp.int32, (ny, LANES), 1)
    steps = nx // planes

    def copies(t, slot):
        at = pl.ds(t * planes, planes)
        return [
            pltpu.make_async_copy(f_hbm.at[at], filled.at[slot], sem.at[slot, 0]),
            pltpu.make_async_copy(o_hbm.at[at], seen.at[slot], sem.at[slot, 1]),
        ]

    def writing(t):
        return pltpu.make_async_copy(out.at[t % 2], out_hbm.at[pl.ds(t * planes, planes)], out_sem.at[t % 2])

    def ahead(t):
        for x in range(t * planes, (t + 1) * planes, ROWS):
            halo_rows(adj, x, y_low[pl.ds(x, ROWS), :], y_high[pl.ds(x, ROWS), :])
        m_low, m_high = z_low[...], one_back(z_high[...])

        def gather(i, carry):
            x = t * planes + i
            beside = columns(m_low, m_high, x, lane)
            _, sums = weighted(adj, x + 1, lane, beside, beside)
            return carry, [(inflow, (h, i), 0.1 * sums[h]) for h in range(count)]

        over(planes, planes, gather)

    def body(t, slot):
        if t >= 2:
            writing(t - 2).wait()

        def plane(i, carry):
            x = t * planes + i
            stores = []
            for h in range(count):
                weight = kept[h, x]
                centre = adj[h, x + 1, ROWS : ROWS + ny, :]
                source = filled[slot, i, :, run(h)].astype(F32) - seen[slot, i, :, run(h)].astype(F32)
                value = centre * weight + (inflow[h, i] + source)
                stores.append((out, (slot, i, slice(None), run(h)), jnp.where(weight == SOLID, 0.0, value)))
            return carry, stores

        over(planes, unroll, plane)
        writing(t).start()

    rotating(steps, copies, body, ahead)
    writing(steps - 2).wait()
    writing(steps - 1).wait()


def last_step(adjoint, kept, filled, seen, halo, after, planes=16, unroll=8):
    count, nx, ny, lanes = kept.shape
    nz = count * lanes
    voxels = nx * ny * nz
    return pl.pallas_call(
        functools.partial(last_kernel, planes, unroll),
        in_specs=[HBM, HBM] + [VMEM] * 6 + [ANY],
        out_specs=[HBM, VMEM],
        out_shape=[jax.ShapeDtypeStruct((nx, ny, nz), F32), pltpu.VMEM(adjoint.shape, F32)],
        scratch_shapes=[
            pltpu.VMEM((2, planes, ny, nz), jnp.bfloat16),
            pltpu.VMEM((2, planes, ny, nz), jnp.bfloat16),
            pltpu.VMEM((2, planes, ny, nz), F32),
            pltpu.VMEM((count, planes, ny, lanes), F32),
            pltpu.SemaphoreType.DMA((2, 2)),
            pltpu.SemaphoreType.DMA((2,)),
        ],
        input_output_aliases={7: 1},
        compiler_params=pltpu.CompilerParams(vmem_limit_bytes=VMEM_LIMIT),
        cost_estimate=pl.CostEstimate(flops=20 * voxels, bytes_accessed=8 * voxels, transcendentals=0),
        name="last_step",
    )(*in_hbm(filled, seen), *in_vmem(kept), *halo, *in_vmem(adjoint), after)[0]


def add_kernel(n_parts, n_after, unroll, *refs):
    parts, outs = refs[:n_parts], refs[n_parts + n_after :]
    planes = outs[0].shape[0]

    def body(i, carry):
        stores = []
        for k, out in enumerate(outs):
            total = parts[0][k * planes + i]
            for part in parts[1:]:
                total = total + part[k * planes + i]
            stores.append((out, (i,), total))
        return carry, stores

    over(planes, unroll, body)


def add(parts, after, pieces, name, unroll=2):
    planes, ny, nz = parts[0].shape
    shape = jax.ShapeDtypeStruct((planes // pieces, ny, nz), F32)
    size = planes * ny * nz
    return pl.pallas_call(
        functools.partial(add_kernel, len(parts), len(after), unroll),
        in_specs=[VMEM] * len(parts) + [ANY] * len(after),
        out_specs=[VMEM] * pieces,
        out_shape=[shape] * pieces,
        compiler_params=pltpu.CompilerParams(vmem_limit_bytes=VMEM_LIMIT),
        cost_estimate=pl.CostEstimate(flops=size * len(parts), bytes_accessed=4 * size, transcendentals=0),
        name=name,
    )(*parts, *after)


def join_kernel(unroll, low, high, low_got, high_got, low_out, high_out):
    planes = low_got.shape[0]

    def body(i, carry):
        return carry, [
            (out, (((part + turned) % 2) * planes + i,), base[planes + i] if part else base[i] + got[i])
            for base, got, out, turned in ((low, low_got, low_out, 0), (high, high_got, high_out, 1))
            for part in (0, 1)
        ]

    over(planes, unroll, body)


def join(low, high, low_got, high_got, unroll=2):
    size = low.size
    return pl.pallas_call(
        functools.partial(join_kernel, unroll),
        in_specs=[VMEM] * 4,
        out_specs=[VMEM] * 2,
        out_shape=[jax.ShapeDtypeStruct(low.shape, F32)] * 2,
        compiler_params=pltpu.CompilerParams(vmem_limit_bytes=VMEM_LIMIT),
        cost_estimate=pl.CostEstimate(flops=size, bytes_accessed=4 * size, transcendentals=0),
        name="join",
    )(low, high, low_got, high_got)


def exchange(y_low, y_high, z_low, z_high):
    received = []
    for axis, low, high in (("gy", y_low, y_high), ("gz", z_low, z_high)):
        count = lax.axis_size(axis)
        up = [(i, i + 1) for i in range(count - 1)]
        down = [(i + 1, i) for i in range(count - 1)]
        received += [lax.ppermute(high, axis, up), lax.ppermute(low, axis, down)]
    return tuple(received)


def places(ring, pairs, share, order):
    rank = lax.axis_index("exp")
    row, half = rank // pairs, rank % pairs
    return [
        (((row + turn) % ring) * pairs + (half + swap) % pairs) * share + part * (share // 2)
        for turn, swap, part in order
    ]


def orders(ring):
    cross = [(turn, 1, 1) for turn in range(ring)]
    far = [(2, 1, 0), (2, 0, 0)]
    near = [(1, 1, 0), (1, 0, 0), (3, 0, 0), (3, 1, 0)]
    own = [(0, 1, 0), (0, 0, 0)] + [(turn, 0, 1) for turn in range(ring)]
    return cross + far, near + own


def shards(ring, adjoint_final, concentration, observed, capacity, pore_mask, feed_index, feed_affinity):
    ranks = lax.axis_size("exp")
    pairs = ranks // ring
    adjoint = adjoint_final[0]
    nx, ny, nz = adjoint.shape
    share = nx // ranks
    planes = share // 2
    filled = concentration.reshape(-1, ny, nz)
    seen = observed.reshape(-1, ny, nz)

    def send(value, turn, swap):
        perm = [
            (r * pairs + h, ((r + turn) % ring) * pairs + (h + swap) % pairs) for r in range(ring) for h in range(pairs)
        ]
        return lax.ppermute(value, "exp", perm)

    scalars = (feed_index, feed_affinity)
    at = [functools.partial(places, ring, pairs, share, order) for order in orders(ring)]
    fields = (capacity, filled, seen)

    masked, wide, *outer = faces(adjoint, pore_mask)
    halo = exchange(*outer)
    state = (masked, weigh(wide))
    state, (cross, far_s, far_k) = stage(scalars, fields, halo, state, at[0], (4, 1, 1), planes, UNROLL, "early")
    crossed = send(cross, 0, 1)
    got_s, got_k = send(far_s, 1, 0), send(far_k, 3, 0)
    (_, kept, next_adjoint, *next_faces), (up, down, own_p, own_q) = stage(
        scalars, fields, halo, state, at[1], (2, 2, 2, 4), planes, UNROLL, "late"
    )
    up, down = join(up, down, got_s, got_k)
    from_low, from_high = send(up, 1, 0), send(down, 3, 0)
    face_halo = exchange(*next_faces)

    totals_q = add([own_q, crossed], face_halo[:1] + face_halo[2:], ring, "add_q")
    parts_q = [send(totals_q[turn], turn, 0) for turn in (2, 1, 3)]
    total_s, total_k = add([own_p, from_low, from_high], totals_q[:1], 2, "add_p")
    last_p = send(total_s, 0, 1)
    adjoint_first = last_step(next_adjoint, kept, filled, seen, face_halo, total_k)

    sum_q = totals_q[0] + parts_q[0] + parts_q[1] + parts_q[2]
    return adjoint_first[None], jnp.concatenate([total_k + last_p, sum_q], 0)


def solution(mesh):
    in_specs = (
        P("exp", None, "gy", "gz"),
        P(None, "exp", None, "gy", "gz"),
        P(None, "exp", None, "gy", "gz"),
        P(None, "gy", "gz"),
        P(None, "gy", "gz"),
        P("exp"),
        P(),
    )
    out_specs = (P("exp", None, "gy", "gz"), P("exp", "gy", "gz"))
    return jax.shard_map(
        functools.partial(shards, 4), mesh=mesh, in_specs=in_specs, out_specs=out_specs, check_vma=False
    )
```
